32 devices in a mesh: dp: 8 (over y, x, core), tensor: 4 (over z).
Axes of the slice: x: 2, y: 2, z: 4, core: 2. Of those that a mesh axis runs over, the one named last changes fastest.
Arguments:
- queries: bfloat16 [384, 5, 8192], P('dp', None, 'tensor'), may hold values from -6 to 6
- new_keys: bfloat16 [384, 5, 1024], P('dp', None, 'tensor'), may hold values from -6 to 6
- new_values: bfloat16 [384, 5, 1024], P('dp', None, 'tensor'), may hold values from -6 to 6
- key_cache: bfloat16 [384, 256, 1024], P('dp', None, 'tensor'), may hold values from -6 to 6
- value_cache: bfloat16 [384, 256, 1024], P('dp', None, 'tensor'), may hold values from -6 to 6
- cache_lengths: int32 [384], P('dp'), may hold values from 2 to 256, as said below
- accepted: int32 [384], P('dp'), may hold values from 0 to 4
- head_weight: bfloat16 [8192, 32768], P('tensor', 'dp'), may hold values from -1.3203125 to 1.3203125
Outputs:
- drafter_logits: float32 [384, 32768], P('tensor', 'dp')
The draws below stay inside these ranges and needn't reach their ends.
Inputs may be any that keep to these rules, and one draw needn't show every extreme that they name: `cache_lengths`: row 0 holds 256 valid slots.
All inputs are finite; a program needn't handle non-finite values.
Results may differ from the reference program's by a relative error of at most 0.015.
Values may be sent and summed in bfloat16 or wider, within the bound.
No kernel may reach another device: no remote copies, remote signals or barrier semaphores. Data moves between devices by JAX's collectives and lax.ppermute only.
A program may use at most 128 MiB of HBM per device.

```python
import jax
import jax.numpy as jnp
from jax import lax

D = 8192
HEADS = 64
KV_HEADS = 8
HEAD_DIM = 128
VOCAB = 32768
DRAFT = 5
ROWS_DEV = 48
CACHE = 256
ROWS = 384
N_TENSOR = 4


def draw_queries(key, part):
    values = jnp.clip(jax.random.normal(jax.random.fold_in(key, 1), (ROWS, DRAFT, D)), -6.0, 6.0)
    return values.astype(jnp.bfloat16)


def draw_key_cache(key, part):
    values = jnp.clip(jax.random.normal(jax.random.fold_in(key, 2), (ROWS, CACHE, KV_HEADS * HEAD_DIM)), -6.0, 6.0)
    return values.astype(jnp.bfloat16)


def draw_cache_lengths(key, part):
    base = jax.random.randint(jax.random.fold_in(key, 5), (ROWS,), 0, CACHE - 1)
    factor = jax.random.randint(jax.random.fold_in(key, 6), (ROWS // ROWS_DEV,), 1, 5)
    factor = jnp.repeat(factor, ROWS_DEV)
    lengths = 2 + base * factor // 4
    return lengths.at[0].set(CACHE).astype(jnp.int32)


def set_ends(result, own_key, smallest, largest):
    spot = [jax.random.randint(jax.random.fold_in(own_key, axis), (), 0, length) for axis, length in enumerate(result.shape)]
    longest = result.shape.index(max(result.shape))
    beside = spot[:longest] + [(spot[longest] + 1) % result.shape[longest]] + spot[longest + 1:]
    return result.at[tuple(spot)].set(smallest).at[tuple(beside)].set(largest)


def shard_levels(stream_key, dims, pieces, smallest, high):
    level, own = 1.0, jax.random.fold_in(stream_key, 6)
    for dim, blocks in pieces:
        draws = jnp.exp(jax.random.uniform(jax.random.fold_in(own, dim), (blocks,), jnp.float32, smallest / len(pieces), high / len(pieces)))
        level = level * jnp.repeat(draws, dims[dim] // blocks).reshape([-1 if axis == dim else 1 for axis in range(len(dims))])
    return level


def noise(own_key, dims, width, bound, cuts=(), held_as=jnp.bfloat16):
    level = shard_levels(own_key, dims, cuts, -0.22, 0.18) if cuts else 1.0
    values = jax.random.normal(own_key, dims, jnp.float32) * width * level
    return jnp.minimum(jnp.maximum(values, -bound), bound).astype(held_as)


def setup_inputs(seed: int = 0) -> dict:
    streams_of = jax.random.split(jax.random.key(seed), 9)
    queries = draw_queries(jax.random.fold_in(streams_of[8], 71), 0)
    new_keys = noise(streams_of[1], (ROWS, DRAFT, KV_HEADS * HEAD_DIM), 1.0, 6.0, ((0, 8), (2, 4)))
    new_values = noise(streams_of[2], (ROWS, DRAFT, KV_HEADS * HEAD_DIM), 1.0, 6.0, ((0, 8), (2, 4)))
    key_cache = draw_key_cache(jax.random.fold_in(streams_of[8], 71), 0)
    value_cache = noise(streams_of[4], (ROWS, CACHE, KV_HEADS * HEAD_DIM), 1.0, 6.0, ((0, 8), (2, 4)))
    cache_lengths = draw_cache_lengths(jax.random.fold_in(streams_of[8], 71), 0)
    accepted = set_ends(jax.random.randint(streams_of[6], (ROWS,), 0, DRAFT), jax.random.fold_in(streams_of[6], 1), 0, DRAFT - 1).astype(jnp.int32)
    head_weight = noise(streams_of[7], (D, VOCAB), (20.0 * D ** -0.5), 1.3203125, ((0, 4), (1, 8)))
    return {"queries": queries, "new_keys": new_keys, "new_values": new_values, "key_cache": key_cache, "value_cache": value_cache, "cache_lengths": cache_lengths, "accepted": accepted, "head_weight": head_weight}


def verify(queries, new_keys, new_values, key_cache, value_cache, cache_lengths):
    row_count = queries.shape[0]
    sharing = HEADS // KV_HEADS
    query_heads = queries.astype(jnp.float32).reshape(row_count, DRAFT, KV_HEADS, sharing, HEAD_DIM)
    past_keys = key_cache.astype(jnp.float32).reshape(row_count, CACHE, KV_HEADS, HEAD_DIM)
    past_values = value_cache.astype(jnp.float32).reshape(row_count, CACHE, KV_HEADS, HEAD_DIM)
    fresh_keys = new_keys.astype(jnp.float32).reshape(row_count, DRAFT, KV_HEADS, HEAD_DIM)
    fresh_values = new_values.astype(jnp.float32).reshape(row_count, DRAFT, KV_HEADS, HEAD_DIM)
    scaling = HEAD_DIM ** -0.5
    past_scores = jnp.einsum("bpgjd,blgd->bpgjl", query_heads, past_keys) * scaling
    fresh_scores = jnp.einsum("bpgjd,bqgd->bpgjq", query_heads, fresh_keys) * scaling
    past_mask = (jnp.arange(CACHE, dtype=jnp.int32)[None, :] < cache_lengths[:, None])[:, None, None, None, :]
    fresh_mask = (jnp.arange(DRAFT)[None, :] <= jnp.arange(DRAFT)[:, None])[None, :, None, None, :]
    lowest = -1e30
    past_masked = jnp.where(past_mask, past_scores, lowest)
    fresh_masked = jnp.where(fresh_mask, fresh_scores, lowest)
    peaks = jnp.maximum(jnp.max(past_masked, axis=-1, keepdims=True), jnp.max(fresh_masked, axis=-1, keepdims=True))
    past_exp = jnp.exp(past_masked - peaks)
    fresh_exp = jnp.exp(fresh_masked - peaks)
    totals = jnp.sum(past_exp, axis=-1, keepdims=True) + jnp.sum(fresh_exp, axis=-1, keepdims=True)
    past_weights = lax.optimization_barrier((past_exp / totals).astype(jnp.bfloat16)).astype(jnp.float32)
    fresh_weights = lax.optimization_barrier((fresh_exp / totals).astype(jnp.bfloat16)).astype(jnp.float32)
    mixed = jnp.einsum("bpgjl,blgd->bpgjd", past_weights, past_values)
    mixed = mixed + jnp.einsum("bpgjq,bqgd->bpgjd", fresh_weights, fresh_values)
    return mixed.astype(jnp.bfloat16).reshape(row_count, DRAFT, D)


def reference(queries, new_keys, new_values, key_cache, value_cache, cache_lengths, accepted, head_weight):
    blocks = ROWS // ROWS_DEV

    def stacked(array):
        return array.reshape((blocks, ROWS_DEV) + array.shape[1:])

    def one_block(inputs):
        return verify(*inputs)

    attended = lax.map(one_block, (stacked(queries), stacked(new_keys), stacked(new_values), stacked(key_cache), stacked(value_cache), stacked(cache_lengths)))
    attended = attended.reshape(ROWS, DRAFT, D)
    picked = jnp.take_along_axis(attended, accepted.astype(jnp.int32)[:, None, None], axis=1)[:, 0, :]
    slices = picked.reshape(ROWS, N_TENSOR, D // N_TENSOR)
    head_parts = head_weight.reshape(N_TENSOR, D // N_TENSOR, VOCAB)

    def add_part(shard, total):
        features = lax.dynamic_index_in_dim(slices, shard, 1, keepdims=False)
        weights = lax.dynamic_index_in_dim(head_parts, shard, 0, keepdims=False)
        part = jnp.dot(features, weights, preferred_element_type=jnp.float32)
        part = lax.optimization_barrier(part.astype(jnp.bfloat16))
        return total + part.astype(jnp.float32)

    return lax.fori_loop(0, N_TENSOR, add_part, jnp.zeros((ROWS, VOCAB), jnp.float32))
```

```python
import functools

import jax
import jax.numpy as jnp
from jax import lax
from jax.experimental import pallas as pl
from jax.experimental.pallas import tpu as pltpu
from jax.sharding import PartitionSpec as P

HEAD_DIM = 128
BLOCK = 16
CHUNK = 4
LOWEST = -1e30


def attend_kernel(
    first, rows, lengths, accepted, queries, new_keys, new_values, key_cache, value_cache,
    picked, q_buf, nk_buf, nv_buf, k_buf, v_buf, spread, mixed, small_sems, k_sems, v_sems,
):
    draft, _, query_cols = q_buf.shape
    cache_len, key_cols = k_buf.shape[1:]
    groups, heads = key_cols // HEAD_DIM, query_cols // HEAD_DIM
    sharing = heads // groups
    scaling = HEAD_DIM ** (-0.5)
    own = pl.ds(first, rows)
    small = [
        pltpu.make_async_copy(src.at[:, own], dst, small_sems.at[n])
        for n, (src, dst) in enumerate(((queries, q_buf), (new_keys, nk_buf), (new_values, nv_buf)))
    ]
    keys, values = [
        [
            pltpu.make_async_copy(src.at[pl.ds(first + at, CHUNK)], dst.at[pl.ds(at, CHUNK)], sems.at[at // CHUNK])
            for at in range(0, rows, CHUNK)
        ]
        for src, dst, sems in ((key_cache, k_buf, k_sems), (value_cache, v_buf, v_sems))
    ]
    for copy in small:
        copy.start()
    for start in range(0, rows // CHUNK, BLOCK // CHUNK):
        for copy in keys[start : start + BLOCK // CHUNK] + values[start : start + BLOCK // CHUNK]:
            copy.start()
    for copy in small:
        copy.wait()
    nt = (((1,), (1,)), ((), ()))
    for block in range(0, rows, BLOCK):
        here = pl.ds(block, BLOCK)
        row = lax.broadcasted_iota(jnp.int32, (BLOCK, HEAD_DIM), 0)
        chosen = jnp.zeros((BLOCK, HEAD_DIM), jnp.int32)
        for r in range(BLOCK):
            chosen = jnp.where(row == r, accepted[first + block + r], chosen)
        for h in range(heads):
            cols = pl.ds(h * HEAD_DIM, HEAD_DIM)
            query = q_buf[0, here, cols].astype(jnp.float32)
            for p in range(1, draft):
                query = jnp.where(chosen == p, q_buf[p, here, cols].astype(jnp.float32), query)
            spread[:, h, :] = query
        query = spread[...].reshape(BLOCK * heads, HEAD_DIM)
        group = lax.rem(lax.broadcasted_iota(jnp.int32, query.shape, 0), heads) // sharing
        query = jnp.concatenate([jnp.where(group == g, query, 0.0) for g in range(groups)], axis=1)
        query = query.astype(jnp.bfloat16)
        fresh_keys = nk_buf[:, here, :].reshape(draft * BLOCK, key_cols)
        fresh_values = nv_buf[:, here, :].reshape(draft * BLOCK, key_cols)
        fresh = lax.dot_general(query, fresh_keys, nt, preferred_element_type=jnp.float32) * scaling
        slot = lax.broadcasted_iota(jnp.int32, (heads, draft * BLOCK), 1)
        lane = lax.broadcasted_iota(jnp.int32, (heads, cache_len), 1)
        weights, fresh_weights = [], []
        for r in range(BLOCK):
            if r % CHUNK == 0:
                keys[(block + r) // CHUNK].wait()
            mine = slice(r * heads, (r + 1) * heads)
            past = lax.dot_general(query[mine], k_buf[block + r], nt, preferred_element_type=jnp.float32) * scaling
            past = jnp.where(lane < lengths[first + block + r], past, LOWEST)
            open_slot = (lax.rem(slot, BLOCK) == r) & (slot // BLOCK <= accepted[first + block + r])
            fresh_r = jnp.where(open_slot, fresh[mine], LOWEST)
            peak = jnp.maximum(jnp.max(past, axis=1, keepdims=True), jnp.max(fresh_r, axis=1, keepdims=True))
            past, fresh_r = jnp.exp(past - peak), jnp.exp(fresh_r - peak)
            total = jnp.sum(past, axis=1, keepdims=True) + jnp.sum(fresh_r, axis=1, keepdims=True)
            weights.append((past / total).astype(jnp.bfloat16))
            fresh_weights.append((fresh_r / total).astype(jnp.bfloat16))
        fresh = jnp.dot(jnp.concatenate(fresh_weights, axis=0), fresh_values, preferred_element_type=jnp.float32)
        own_group = lax.broadcasted_iota(jnp.int32, (heads, HEAD_DIM), 0) // sharing
        for r in range(BLOCK):
            if r % CHUNK == 0:
                values[(block + r) // CHUNK].wait()
            result = jnp.dot(weights[r], v_buf[block + r], preferred_element_type=jnp.float32)
            result = result + fresh[r * heads : (r + 1) * heads]
            kept = result[:, :HEAD_DIM]
            for g in range(1, groups):
                kept = jnp.where(own_group == g, result[:, g * HEAD_DIM : (g + 1) * HEAD_DIM], kept)
            mixed[r] = kept
        for h in range(heads):
            picked[here, pl.ds(h * HEAD_DIM, HEAD_DIM)] = mixed[:, h, :].astype(jnp.bfloat16)


def attend(first, rows, lengths, accepted, queries, new_keys, new_values, key_cache, value_cache):
    draft, _, query_cols = queries.shape
    _, cache_len, key_cols = key_cache.shape
    heads = query_cols // HEAD_DIM
    smem, anywhere = pl.BlockSpec(memory_space=pltpu.SMEM), pl.BlockSpec(memory_space=pl.ANY)
    cached = 2 * rows * cache_len * key_cols
    return pl.pallas_call(
        functools.partial(attend_kernel, first, rows),
        out_shape=jax.ShapeDtypeStruct((rows, query_cols), jnp.bfloat16),
        in_specs=[smem, smem] + [anywhere] * 5,
        out_specs=pl.BlockSpec(memory_space=pltpu.VMEM),
        scratch_shapes=[
            pltpu.VMEM((draft, rows, query_cols), jnp.bfloat16),
            pltpu.VMEM((draft, rows, key_cols), jnp.bfloat16),
            pltpu.VMEM((draft, rows, key_cols), jnp.bfloat16),
            pltpu.VMEM((rows, cache_len, key_cols), jnp.bfloat16),
            pltpu.VMEM((rows, cache_len, key_cols), jnp.bfloat16),
            pltpu.VMEM((BLOCK, heads, HEAD_DIM), jnp.float32),
            pltpu.VMEM((BLOCK, heads, HEAD_DIM), jnp.float32),
            pltpu.SemaphoreType.DMA((3,)),
            pltpu.SemaphoreType.DMA((rows // CHUNK,)),
            pltpu.SemaphoreType.DMA((rows // CHUNK,)),
        ],
        compiler_params=pltpu.CompilerParams(vmem_limit_bytes=40 << 20),
        cost_estimate=pl.CostEstimate(flops=2 * heads * cached, bytes_accessed=2 * cached, transcendentals=rows * heads * cache_len),
    )(lengths, accepted, queries, new_keys, new_values, key_cache, value_cache)


def head_kernel(count, *refs):
    pieces, weight, part, features = refs[:count], refs[count], refs[count + 1], refs[count + 2]

    @pl.when(pl.program_id(0) == 0)
    def _():
        at = 0
        for piece in pieces:
            features[pl.ds(at, piece.shape[0]), :] = piece[...]
            at += piece.shape[0]

    part[...] = jnp.dot(features[...], weight[...], preferred_element_type=jnp.float32).astype(jnp.bfloat16)


def head(pieces, weight, tile=512):
    depth, cols = weight.shape
    rows = sum(piece.shape[0] for piece in pieces)
    return pl.pallas_call(
        functools.partial(head_kernel, len(pieces)),
        grid=(cols // tile,),
        out_shape=jax.ShapeDtypeStruct((rows, cols), jnp.bfloat16),
        in_specs=[pl.BlockSpec(piece.shape, lambda n: (0, 0)) for piece in pieces]
        + [pl.BlockSpec((depth, tile), lambda n: (0, n))],
        out_specs=pl.BlockSpec((rows, tile), lambda n: (0, n)),
        scratch_shapes=[pltpu.VMEM((rows, depth), jnp.bfloat16)],
        compiler_params=pltpu.CompilerParams(vmem_limit_bytes=40 << 20),
        cost_estimate=pl.CostEstimate(
            flops=2 * rows * depth * cols, bytes_accessed=2 * (depth * cols + rows * depth + rows * cols), transcendentals=0
        ),
    )(*pieces, weight)


def gather(block, dp):
    if dp != 8:
        return [lax.all_gather(block, "dp", axis=0, tiled=True)]

    def swap(array, bits):
        return lax.ppermute(array, "dp", [(i, i ^ bits) for i in range(dp)])

    beside, below, across = swap(block, 2), swap(block, 4), swap(block, 6)
    return [block, swap(block, 1), beside, swap(beside, 1), below, swap(below, 1), across, swap(across, 1)]


def shards(
    tensor, dp, queries, new_keys, new_values, key_cache, value_cache, cache_lengths, accepted, head_weight
):
    rows_dev = queries.shape[0]
    queries, new_keys, new_values = [jnp.transpose(a, (1, 0, 2)) for a in (queries, new_keys, new_values)]
    me, place = lax.axis_index("tensor"), lax.axis_index("dp")
    sources = dp // tensor
    paired = dp == 8 and tensor == 4

    bounds = [(0, BLOCK), (BLOCK, rows_dev - BLOCK)]
    parts = []
    for first, rows in bounds:
        picked = attend(first, rows, cache_lengths, accepted, queries, new_keys, new_values, key_cache, value_cache)
        pieces = gather(picked, dp)
        parts.append(head(pieces, head_weight))

    def term(part, shard):
        size = part.shape[0] // tensor
        if paired:
            shard = shard ^ (place // sources)
        return lax.dynamic_slice_in_dim(part, shard * size, size, axis=0)

    def add(part, shard, arrived):
        mine = term(part, jnp.clip(shard, 0, tensor - 1))
        if arrived is None:
            return mine
        return (mine.astype(jnp.float32) + arrived.astype(jnp.float32)).astype(jnp.bfloat16)

    ups, downs = [None] * len(parts), [None] * len(parts)
    for step in range(1, tensor):
        up = [(z, z + 1) for z in range(step)]
        down = [(tensor - 1 - z, tensor - 2 - z) for z in range(step)]
        for n, part in enumerate(parts):
            ups[n] = lax.ppermute(add(part, tensor - step + me, ups[n]), "tensor", up)
            downs[n] = lax.ppermute(add(part, step - tensor + me, downs[n]), "tensor", down)

    results = []
    for part, up, down in zip(parts, ups, downs):
        total = term(part, me).astype(jnp.float32) + up.astype(jnp.float32) + down.astype(jnp.float32)
        total = total.reshape(sources, -1, total.shape[-1])
        if paired:
            total = jnp.where(place % 2 == 1, total[::-1], total)
        results.append(total)
    total = jnp.concatenate(results, axis=1)
    return total.reshape(-1, total.shape[-1])


def solution(mesh):
    in_specs = (
        P("dp", None, "tensor"),
        P("dp", None, "tensor"),
        P("dp", None, "tensor"),
        P("dp", None, "tensor"),
        P("dp", None, "tensor"),
        P("dp"),
        P("dp"),
        P("tensor", "dp"),
    )
    out_specs = P("tensor", "dp")
    body = functools.partial(shards, mesh.shape["tensor"], mesh.shape["dp"])
    return jax.shard_map(body, mesh=mesh, in_specs=in_specs, out_specs=out_specs, check_vma=False)
```

```python
import functools
import math

import jax
import jax.numpy as jnp
from jax import lax
from jax.experimental import pallas as pl
from jax.experimental.pallas import tpu as pltpu
from jax.sharding import PartitionSpec as P

HEAD_DIM = 128
BLOCK = 16
CHUNK = 16
LOWEST = -1e30


def attend_kernel(first, rows, before, *refs):
    all_lengths, all_accepted, queries, new_keys, new_values, key_cache, value_cache, *refs = refs
    *earlier, picked = refs[:-12]
    lengths, accepted, q_buf, nk_buf, nv_buf, k_buf, v_buf, spread, mixed, small_sems, k_sems, v_sems = refs[-12:]
    draft, _, query_cols = q_buf.shape
    cache_len, key_cols = k_buf.shape[1:]
    groups, heads = key_cols // HEAD_DIM, query_cols // HEAD_DIM
    sharing = heads // groups
    scaling = HEAD_DIM ** (-0.5)
    own = pl.ds(first, rows)
    small = [(all_accepted, accepted), (all_lengths, lengths)]
    small += [(src.at[:, own], dst) for src, dst in ((queries, q_buf), (new_keys, nk_buf), (new_values, nv_buf))]
    small = [pltpu.make_async_copy(src, dst, small_sems.at[n]) for n, (src, dst) in enumerate(small)]
    keys, values = [
        [
            pltpu.make_async_copy(src.at[pl.ds(first + at, CHUNK)], dst.at[pl.ds(at, CHUNK)], sems.at[at // CHUNK])
            for at in range(0, rows, CHUNK)
        ]
        for src, dst, sems in ((key_cache, k_buf, k_sems), (value_cache, v_buf, v_sems))
    ]
    for copy in small:
        copy.start()
    for start in range(0, rows // CHUNK, BLOCK // CHUNK):
        for copy in keys[start : start + BLOCK // CHUNK] + values[start : start + BLOCK // CHUNK]:
            copy.start()
    if before:
        picked[:before, :] = earlier[0][...]
    for copy in small:
        copy.wait()
    lanes = BLOCK * heads
    nt, tn = (((1,), (1,)), ((), ())), (((0,), (0,)), ((), ()))
    lane_row = lax.broadcasted_iota(jnp.int32, (1, lanes), 1) // heads
    for block in range(0, rows, BLOCK):
        here = pl.ds(block, BLOCK)
        row = lax.broadcasted_iota(jnp.int32, (BLOCK, HEAD_DIM), 0)
        chosen = jnp.zeros((BLOCK, HEAD_DIM), jnp.int32)
        length, last = jnp.zeros((1, lanes), jnp.int32), jnp.zeros((1, lanes), jnp.int32)
        for r in range(BLOCK):
            chosen = jnp.where(row == r, accepted[first + block + r], chosen)
            last = jnp.where(lane_row == r, accepted[first + block + r], last)
            length = jnp.where(lane_row == r, lengths[first + block + r], length)
        for h in range(heads):
            cols = pl.ds(h * HEAD_DIM, HEAD_DIM)
            query = q_buf[0, here, cols].astype(jnp.float32)
            for p in range(1, draft):
                query = jnp.where(chosen == p, q_buf[p, here, cols].astype(jnp.float32), query)
            spread[:, h, :] = query
            wide = []
        for g in range(groups):
            keep = lax.broadcasted_iota(jnp.int32, spread.shape, 1) // sharing == g
            wide.append(jnp.where(keep, spread[...], 0.0).reshape(lanes, HEAD_DIM))
        query = jnp.concatenate(wide, axis=1).astype(jnp.bfloat16)

        fresh_keys = nk_buf[:, here, :].reshape(draft * BLOCK, key_cols)
        fresh_values = nv_buf[:, here, :].reshape(draft * BLOCK, key_cols)
        fresh = lax.dot_general(fresh_keys, query, nt, preferred_element_type=jnp.float32) * scaling
        slot = lax.broadcasted_iota(jnp.int32, fresh.shape, 0)
        fresh = jnp.where((slot % BLOCK == lane_row) & (slot // BLOCK <= last), fresh, LOWEST)
        past = []
        for lane in range(0, lanes, HEAD_DIM):
            part = None
            for r in range(lane // heads, (lane + HEAD_DIM) // heads):
                if r % CHUNK == 0:
                    keys[(block + r) // CHUNK].wait()
                score = lax.dot_general(
                    k_buf[block + r], query[lane : lane + HEAD_DIM], nt, preferred_element_type=jnp.float32
                )
                part = score if part is None else jnp.where(lane_row[:, lane : lane + HEAD_DIM] == r, score, part)
            past.append(part)
        past = jnp.concatenate(past, axis=1) * scaling
        past = jnp.where(lax.broadcasted_iota(jnp.int32, past.shape, 0) < length, past, LOWEST)
        peak = jnp.maximum(jnp.max(past, axis=0, keepdims=True), jnp.max(fresh, axis=0, keepdims=True))
        past, fresh = jnp.exp(past - peak), jnp.exp(fresh - peak)
        total = jnp.sum(past, axis=0, keepdims=True) + jnp.sum(fresh, axis=0, keepdims=True)
        weights = jnp.transpose(past / total)
        fresh = (fresh / total).astype(jnp.bfloat16)
        fresh = lax.dot_general(fresh, fresh_values, tn, preferred_element_type=jnp.float32)
        own_group = lax.broadcasted_iota(jnp.int32, (heads, HEAD_DIM), 0) // sharing
        for r in range(BLOCK):
            if r % CHUNK == 0:
                values[(block + r) // CHUNK].wait()
            mine = slice(r * heads, (r + 1) * heads)
            result = jnp.dot(weights[mine].astype(jnp.bfloat16), v_buf[block + r], preferred_element_type=jnp.float32)
            result = result + fresh[mine]
            kept = result[:, :HEAD_DIM]
            for g in range(1, groups):
                kept = jnp.where(own_group == g, result[:, g * HEAD_DIM : (g + 1) * HEAD_DIM], kept)
            mixed[r] = kept
        for h in range(heads):
            picked[pl.ds(before + block, BLOCK), pl.ds(h * HEAD_DIM, HEAD_DIM)] = mixed[:, h, :].astype(jnp.bfloat16)


def attend(first, rows, arrays, earlier=None, after=None):
    draft, _, query_cols = arrays[2].shape
    _, cache_len, key_cols = arrays[5].shape
    heads = query_cols // HEAD_DIM
    vmem, anywhere = pl.BlockSpec(memory_space=pltpu.VMEM), pl.BlockSpec(memory_space=pl.ANY)
    cached = 2 * rows * cache_len * key_cols
    before = 0 if earlier is None else earlier.shape[0]
    extra = [] if earlier is None else [earlier]
    tokens = [] if after is None else [after]

    def kernel(*refs):
        given = 7 + len(extra)
        attend_kernel(first, rows, before, *refs[:given], *refs[given + len(tokens) :])

    return pl.pallas_call(
        kernel,
        out_shape=jax.ShapeDtypeStruct((before + rows, query_cols), jnp.bfloat16),
        in_specs=[anywhere] * 7 + [vmem] * len(extra) + [anywhere] * len(tokens),
        out_specs=vmem,
        scratch_shapes=[
            pltpu.SMEM(arrays[0].shape, jnp.int32),
            pltpu.SMEM(arrays[1].shape, jnp.int32),
            pltpu.VMEM((draft, rows, query_cols), jnp.bfloat16),
            pltpu.VMEM((draft, rows, key_cols), jnp.bfloat16),
            pltpu.VMEM((draft, rows, key_cols), jnp.bfloat16),
            pltpu.VMEM((rows, cache_len, key_cols), jnp.bfloat16),
            pltpu.VMEM((rows, cache_len, key_cols), jnp.bfloat16),
            pltpu.VMEM((BLOCK, heads, HEAD_DIM), jnp.float32),
            pltpu.VMEM((BLOCK, heads, HEAD_DIM), jnp.float32),
            pltpu.SemaphoreType.DMA((5,)),
            pltpu.SemaphoreType.DMA((rows // CHUNK,)),
            pltpu.SemaphoreType.DMA((rows // CHUNK,)),
        ],
        compiler_params=pltpu.CompilerParams(vmem_limit_bytes=8 << 20),
        cost_estimate=pl.CostEstimate(flops=2 * heads * cached, bytes_accessed=2 * cached, transcendentals=rows * heads * cache_len),
    )(*[pltpu.with_memory_space_constraint(a, pltpu.HBM) for a in arrays], *extra, *tokens)


def head_kernel(count, first, tile, *refs):
    pieces, weight, (part, features, held, sems) = refs[:count], refs[count], refs[-4:]
    copies = [
        pltpu.make_async_copy(weight.at[:, pl.ds(first + at, tile)], held.at[n], sems.at[n])
        for n, at in enumerate(range(0, part.shape[1], tile))
    ]
    for copy in copies:
        copy.start()
    at = 0
    for piece in pieces:
        features[pl.ds(at, piece.shape[0]), :] = piece[...]
        at += piece.shape[0]
    for n, copy in enumerate(copies):
        copy.wait()
        product = jnp.dot(features[...], held[n], preferred_element_type=jnp.float32)
        part[:, pl.ds(n * tile, tile)] = product.astype(jnp.bfloat16)


def head(pieces, weight, first, cols, after=None):
    tokens = [] if after is None else [after]
    depth = weight.shape[0]
    rows = sum(piece.shape[0] for piece in pieces)
    tile = min(512, cols)
    whole = pl.BlockSpec(memory_space=pltpu.VMEM)
    return pl.pallas_call(
        functools.partial(head_kernel, len(pieces), first, tile),
        out_shape=jax.ShapeDtypeStruct((rows, cols), jnp.bfloat16),
        in_specs=[whole] * len(pieces) + [pl.BlockSpec(memory_space=pl.ANY)] * (1 + len(tokens)),
        out_specs=whole,
        scratch_shapes=[
            pltpu.VMEM((rows, depth), jnp.bfloat16),
            pltpu.VMEM((cols // tile, depth, tile), jnp.bfloat16),
            pltpu.SemaphoreType.DMA((cols // tile,)),
        ],
        compiler_params=pltpu.CompilerParams(vmem_limit_bytes=28 << 20),
        cost_estimate=pl.CostEstimate(
            flops=2 * rows * depth * cols, bytes_accessed=2 * (depth * cols + rows * depth + rows * cols), transcendentals=0
        ),
    )(*pieces, pltpu.with_memory_space_constraint(weight, pltpu.HBM), *tokens)


def swap(array, dp, bits):
    return lax.ppermute(array, "dp", [(i, i ^ bits) for i in range(dp)])


def behind(array, other):
    return lax.optimization_barrier((array, other))[0]


def shards(
    tensor, dp, queries, new_keys, new_values, key_cache, value_cache, cache_lengths, accepted, head_weight
):
    rows_dev = queries.shape[0]
    queries, new_keys, new_values = [jnp.transpose(a, (1, 0, 2)) for a in (queries, new_keys, new_values)]
    arrays = (cache_lengths, accepted, queries, new_keys, new_values, key_cache, value_cache)
    me, place = lax.axis_index("tensor"), lax.axis_index("dp")
    sources = dp // tensor
    paired = dp == 8 and tensor == 4
    cols = head_weight.shape[1]
    half = cols // 2

    first = attend(0, BLOCK, arrays)
    middle = attend(BLOCK, BLOCK, arrays, after=first)
    if paired:
        beside = behind(swap(first, dp, 2), middle)
        chips = jnp.concatenate([first, beside])
    rest = attend(2 * BLOCK, rows_dev - 2 * BLOCK, arrays, earlier=middle, after=chips if paired else middle)
    if paired:
        below = behind(swap(chips, dp, 4), rest)
        chips = jnp.concatenate([chips, below])
        pieces = [chips, swap(chips, dp, 1)]
    else:
        pieces = [lax.all_gather(first, "dp", axis=0, tiled=True)]
    spare = swap(rest, dp, 2) if paired else None

    def view(part):
        if paired:
            return part.reshape(2, tensor, -1, part.shape[-1])
        return part.reshape(1, tensor, -1, part.shape[-1])

    def chosen(shard):
        return shard ^ (lax.axis_index("dp") // 2) if paired else shard

    def add_kernel(step, parity, fresh, part, *refs):
        arrived, sent = refs[: 1 - fresh], refs[-1]
        z = lax.axis_index("tensor")
        shard = jnp.where(lax.rem(z, 2) == parity, tensor - step + z, step - tensor + z)
        at = chosen(jnp.clip(shard, 0, tensor - 1))
        if arrived:
            total = part[:, at].astype(jnp.float32) + arrived[0][...].astype(jnp.float32)
            sent[...] = total.astype(jnp.bfloat16)
        else:
            sent[...] = part[:, at]

    def add(part, step, parity, arrived, after):
        shape = part.shape[:1] + part.shape[2:]
        vmem = pl.BlockSpec(memory_space=pltpu.VMEM)
        given = [part] if arrived is None else [part, arrived]
        return pl.pallas_call(
            functools.partial(add_kernel, step, parity, 2 - len(given)),
            out_shape=jax.ShapeDtypeStruct(shape, jnp.bfloat16),
            in_specs=[vmem] * len(given) + [pl.BlockSpec(memory_space=pl.ANY)],
            out_specs=vmem,
            compiler_params=pltpu.CompilerParams(vmem_limit_bytes=8 << 20),
            cost_estimate=pl.CostEstimate(flops=0, bytes_accessed=6 * math.prod(shape), transcendentals=0),
        )(*given, after)

    def links(step, parity):
        up = [(z, z + 1) for z in range(parity, tensor - 1, 2) if z < step]
        down = [(z + 1, z) for z in range(parity, tensor - 1, 2) if tensor - 2 - z < step]
        return up + down

    parts, arrived = {}, {}

    def send(n, step, parity, after):
        if not links(step, parity):
            return after
        value = add(parts[n], step, parity, arrived.get((n, step - 1, 1 - parity)), after)
        arrived[n, step, parity] = lax.ppermute(value, "tensor", links(step, parity))
        return value

    parts[0] = view(head(pieces, head_weight, 0, cols))
    last = parts[0]
    if paired:
        last = send(0, 1, 0, last)
        last = send(0, 2, 0, last)
        chips = jnp.concatenate([rest, behind(spare, last)])
        last = send(0, 2, 1, last)
        chips = jnp.concatenate([chips, behind(swap(chips, dp, 4), last)])
        rest = [chips, swap(chips, dp, 1)]
    else:
        rest = [lax.all_gather(rest, "dp", axis=0, tiled=True)]
    last = parts[1] = view(head(rest, head_weight, 0, half, last))
    if paired:
        order = [(1, 1, 0), (1, 2, 0), (0, 3, 0), (0, 3, 1), None, (2, 1, 0), (2, 2, 0)]
        order += [(1, 2, 1), (1, 3, 1), (1, 3, 0), (2, 2, 1), (2, 3, 0), (2, 3, 1)]
    else:
        order = [None] + [(n, step, parity) for step in range(1, tensor) for n in range(3) for parity in range(2)]
    for entry in order:
        if entry is None:
            last = parts[2] = view(head(rest, head_weight, half, half, last))
        elif entry not in arrived:
            last = send(*entry, last)

    results = []
    for n in range(3):
        part = parts[n]
        total = lax.dynamic_index_in_dim(part, chosen(me), axis=1, keepdims=False).astype(jnp.float32)
        for parity in range(2):
            if (n, tensor - 1, parity) in arrived:
                total = total + arrived[n, tensor - 1, parity].astype(jnp.float32)
        if paired:
            total = jnp.where(place % 2 == 1, total[::-1], total)
        else:
            total = total.reshape(sources, -1, total.shape[-1])
        results.append(total)
    total = jnp.concatenate([results[0], jnp.concatenate(results[1:], axis=2)], axis=1)
    return total.reshape(-1, cols)


def solution(mesh):
    in_specs = (
        P("dp", None, "tensor"),
        P("dp", None, "tensor"),
        P("dp", None, "tensor"),
        P("dp", None, "tensor"),
        P("dp", None, "tensor"),
        P("dp"),
        P("dp"),
        P("tensor", "dp"),
    )
    out_specs = P("tensor", "dp")
    body = functools.partial(shards, mesh.shape["tensor"], mesh.shape["dp"])
    return jax.shard_map(body, mesh=mesh, in_specs=in_specs, out_specs=out_specs, check_vma=False)
```

```python
import functools

import jax
import jax.numpy as jnp
from jax import lax
from jax.experimental import pallas as pl
from jax.experimental.pallas import tpu as pltpu
from jax.sharding import PartitionSpec as P

HEAD_DIM = 128
BLOCK = 16
CHUNK = 16
LOWEST = -1e30
SHORT = pl.CostEstimate(flops=0, bytes_accessed=0, transcendentals=0)


def attend_kernel(first, rows, before, *refs):
    all_lengths, all_accepted, queries, new_keys, new_values, key_cache, value_cache, *refs = refs
    *earlier, picked = refs[:-12]
    lengths, accepted, q_buf, nk_buf, nv_buf, k_buf, v_buf, spread, mixed, small_sems, k_sems, v_sems = refs[-12:]
    draft, _, query_cols = q_buf.shape
    cache_len, key_cols = k_buf.shape[1:]
    groups, heads = key_cols // HEAD_DIM, query_cols // HEAD_DIM
    sharing = heads // groups
    scaling = HEAD_DIM ** (-0.5)
    own = pl.ds(first, rows)
    small = [(all_accepted, accepted), (all_lengths, lengths)]
    small += [(src.at[:, own], dst) for src, dst in ((queries, q_buf), (new_keys, nk_buf), (new_values, nv_buf))]
    small = [pltpu.make_async_copy(src, dst, small_sems.at[n]) for n, (src, dst) in enumerate(small)]
    keys, values = [
        [
            pltpu.make_async_copy(src.at[pl.ds(first + at, CHUNK)], dst.at[pl.ds(at, CHUNK)], sems.at[at // CHUNK])
            for at in range(0, rows, CHUNK)
        ]
        for src, dst, sems in ((key_cache, k_buf, k_sems), (value_cache, v_buf, v_sems))
    ]
    for copy in small:
        copy.start()
    for start in range(0, rows // CHUNK, BLOCK // CHUNK):
        for copy in keys[start : start + BLOCK // CHUNK] + values[start : start + BLOCK // CHUNK]:
            copy.start()
    if before:
        picked[:before, :] = earlier[0][...]
    for copy in small:
        copy.wait()
    lanes = BLOCK * heads
    nt, tn = (((1,), (1,)), ((), ())), (((0,), (0,)), ((), ()))
    lane_row = lax.broadcasted_iota(jnp.int32, (1, lanes), 1) // heads
    for block in range(0, rows, BLOCK):
        here = pl.ds(block, BLOCK)
        row = lax.broadcasted_iota(jnp.int32, (BLOCK, HEAD_DIM), 0)
        chosen = jnp.zeros((BLOCK, HEAD_DIM), jnp.int32)
        length, last = jnp.zeros((1, lanes), jnp.int32), jnp.zeros((1, lanes), jnp.int32)
        for r in range(BLOCK):
            chosen = jnp.where(row == r, accepted[first + block + r], chosen)
            last = jnp.where(lane_row == r, accepted[first + block + r], last)
            length = jnp.where(lane_row == r, lengths[first + block + r], length)
        for h in range(heads):
            cols = pl.ds(h * HEAD_DIM, HEAD_DIM)
            query = q_buf[0, here, cols].astype(jnp.float32)
            for p in range(1, draft):
                query = jnp.where(chosen == p, q_buf[p, here, cols].astype(jnp.float32), query)
            spread[:, h, :] = query
            wide = []
        for g in range(groups):
            keep = lax.broadcasted_iota(jnp.int32, spread.shape, 1) // sharing == g
            wide.append(jnp.where(keep, spread[...], 0.0).reshape(lanes, HEAD_DIM))
        query = jnp.concatenate(wide, axis=1).astype(jnp.bfloat16)

        fresh_keys = nk_buf[:, here, :].reshape(draft * BLOCK, key_cols)
        fresh_values = nv_buf[:, here, :].reshape(draft * BLOCK, key_cols)
        fresh = lax.dot_general(fresh_keys, query, nt, preferred_element_type=jnp.float32) * scaling
        slot = lax.broadcasted_iota(jnp.int32, fresh.shape, 0)
        fresh = jnp.where((slot % BLOCK == lane_row) & (slot // BLOCK <= last), fresh, LOWEST)
        past = []
        for lane in range(0, lanes, HEAD_DIM):
            part = None
            for r in range(lane // heads, (lane + HEAD_DIM) // heads):
                if r % CHUNK == 0:
                    keys[(block + r) // CHUNK].wait()
                score = lax.dot_general(
                    k_buf[block + r], query[lane : lane + HEAD_DIM], nt, preferred_element_type=jnp.float32
                )
                part = score if part is None else jnp.where(lane_row[:, lane : lane + HEAD_DIM] == r, score, part)
            past.append(part)
        past = jnp.concatenate(past, axis=1) * scaling
        past = jnp.where(lax.broadcasted_iota(jnp.int32, past.shape, 0) < length, past, LOWEST)
        peak = jnp.maximum(jnp.max(past, axis=0, keepdims=True), jnp.max(fresh, axis=0, keepdims=True))
        past, fresh = jnp.exp(past - peak), jnp.exp(fresh - peak)
        total = jnp.sum(past, axis=0, keepdims=True) + jnp.sum(fresh, axis=0, keepdims=True)
        weights = jnp.transpose(past / total)
        fresh = (fresh / total).astype(jnp.bfloat16)
        fresh = lax.dot_general(fresh, fresh_values, tn, preferred_element_type=jnp.float32)
        own_group = lax.broadcasted_iota(jnp.int32, (heads, HEAD_DIM), 0) // sharing
        for r in range(BLOCK):
            if r % CHUNK == 0:
                values[(block + r) // CHUNK].wait()
            mine = slice(r * heads, (r + 1) * heads)
            result = jnp.dot(weights[mine].astype(jnp.bfloat16), v_buf[block + r], preferred_element_type=jnp.float32)
            result = result + fresh[mine]
            kept = result[:, :HEAD_DIM]
            for g in range(1, groups):
                kept = jnp.where(own_group == g, result[:, g * HEAD_DIM : (g + 1) * HEAD_DIM], kept)
            mixed[r] = kept
        for h in range(heads):
            picked[pl.ds(before + block, BLOCK), pl.ds(h * HEAD_DIM, HEAD_DIM)] = mixed[:, h, :].astype(jnp.bfloat16)


def attend(first, rows, arrays, earlier=None, after=None):
    draft, _, query_cols = arrays[2].shape
    _, cache_len, key_cols = arrays[5].shape
    heads = query_cols // HEAD_DIM
    vmem, anywhere = pl.BlockSpec(memory_space=pltpu.VMEM), pl.BlockSpec(memory_space=pl.ANY)
    cached = 2 * rows * cache_len * key_cols
    before = 0 if earlier is None else earlier.shape[0]
    extra = [] if earlier is None else [earlier]
    tokens = [] if after is None else [after]

    def kernel(*refs):
        given = 7 + len(extra)
        attend_kernel(first, rows, before, *refs[:given], *refs[given + len(tokens) :])

    return pl.pallas_call(
        kernel,
        out_shape=jax.ShapeDtypeStruct((before + rows, query_cols), jnp.bfloat16),
        in_specs=[anywhere] * 7 + [vmem] * len(extra) + [anywhere] * len(tokens),
        out_specs=vmem,
        scratch_shapes=[
            pltpu.SMEM(arrays[0].shape, jnp.int32),
            pltpu.SMEM(arrays[1].shape, jnp.int32),
            pltpu.VMEM((draft, rows, query_cols), jnp.bfloat16),
            pltpu.VMEM((draft, rows, key_cols), jnp.bfloat16),
            pltpu.VMEM((draft, rows, key_cols), jnp.bfloat16),
            pltpu.VMEM((rows, cache_len, key_cols), jnp.bfloat16),
            pltpu.VMEM((rows, cache_len, key_cols), jnp.bfloat16),
            pltpu.VMEM((BLOCK, heads, HEAD_DIM), jnp.float32),
            pltpu.VMEM((BLOCK, heads, HEAD_DIM), jnp.float32),
            pltpu.SemaphoreType.DMA((5,)),
            pltpu.SemaphoreType.DMA((rows // CHUNK,)),
            pltpu.SemaphoreType.DMA((rows // CHUNK,)),
        ],
        compiler_params=pltpu.CompilerParams(vmem_limit_bytes=8 << 20),
        cost_estimate=SHORT,
    )(*[pltpu.with_memory_space_constraint(a, pltpu.HBM) for a in arrays], *extra, *tokens)


def head_kernel(count, first, tile, *refs):
    pieces, weight, (part, features, held, sems) = refs[:count], refs[count], refs[-4:]
    copies = [
        pltpu.make_async_copy(weight.at[:, pl.ds(first + at, tile)], held.at[n], sems.at[n])
        for n, at in enumerate(range(0, part.shape[1], tile))
    ]
    for copy in copies:
        copy.start()
    at = 0
    for piece in pieces:
        features[pl.ds(at, piece.shape[0]), :] = piece[...]
        at += piece.shape[0]
    for n, copy in enumerate(copies):
        copy.wait()
        product = jnp.dot(features[...], held[n], preferred_element_type=jnp.float32)
        part[:, pl.ds(n * tile, tile)] = product.astype(jnp.bfloat16)


def head(pieces, weight, first, cols, after=None):
    tokens = [] if after is None else [after]
    depth = weight.shape[0]
    rows = sum(piece.shape[0] for piece in pieces)
    tile = min(512, cols)
    whole = pl.BlockSpec(memory_space=pltpu.VMEM)
    return pl.pallas_call(
        functools.partial(head_kernel, len(pieces), first, tile),
        out_shape=jax.ShapeDtypeStruct((rows, cols), jnp.bfloat16),
        in_specs=[whole] * len(pieces) + [pl.BlockSpec(memory_space=pl.ANY)] * (1 + len(tokens)),
        out_specs=whole,
        scratch_shapes=[
            pltpu.VMEM((rows, depth), jnp.bfloat16),
            pltpu.VMEM((cols // tile, depth, tile), jnp.bfloat16),
            pltpu.SemaphoreType.DMA((cols // tile,)),
        ],
        compiler_params=pltpu.CompilerParams(vmem_limit_bytes=28 << 20),
        cost_estimate=SHORT,
    )(*pieces, pltpu.with_memory_space_constraint(weight, pltpu.HBM), *tokens)


def swap(array, dp, bits):
    return lax.ppermute(array, "dp", [(i, i ^ bits) for i in range(dp)])


def behind(array, other):
    return lax.optimization_barrier((array, other))[0]


def shards(
    tensor, dp, queries, new_keys, new_values, key_cache, value_cache, cache_lengths, accepted, head_weight
):
    rows_dev = queries.shape[0]
    queries, new_keys, new_values = [jnp.transpose(a, (1, 0, 2)) for a in (queries, new_keys, new_values)]
    arrays = (cache_lengths, accepted, queries, new_keys, new_values, key_cache, value_cache)
    sources = dp // tensor
    paired = dp == 8 and tensor == 4
    cols = head_weight.shape[1]

    blocks, chips, pieces, last = [], {}, {}, None
    for n in range(rows_dev // BLOCK):
        blocks.append(attend(n * BLOCK, BLOCK, arrays, after=last))
        last = blocks[n]
        if paired:
            chips[n] = swap(blocks[n], dp, 2)
        if paired and n == 1:
            chips[0] = jnp.concatenate([blocks[0], behind(chips[0], last)])
            last = chips[0]

    def along_y(n, after):
        chips[n] = jnp.concatenate([blocks[n], behind(chips[n], after)])

    def along_cores(n, after):
        both = jnp.concatenate([chips[n], behind(swap(chips[n], dp, 4), after)])
        pieces[n] = [both, swap(both, dp, 1)]

    def view(part):
        if paired:
            return part.reshape(2, tensor, -1, part.shape[-1])
        return part.reshape(1, tensor, -1, part.shape[-1])

    def chosen(shard):
        return shard ^ (lax.axis_index("dp") // 2) if paired else shard

    def add_kernel(steps, parity, places, part, *refs):
        refs, sent = list(refs[:-1]), refs[-1]
        z = lax.axis_index("tensor")
        for n, (step, place) in enumerate(zip(steps, places)):
            shard = jnp.where(lax.rem(z, 2) == parity, tensor - step + z, step - tensor + z)
            at = chosen(jnp.clip(shard, 0, tensor - 1))
            if place is None:
                sent[n] = part[:, at]
            else:
                total = part[:, at].astype(jnp.float32) + refs.pop(0)[place].astype(jnp.float32)
                sent[n] = total.astype(jnp.bfloat16)

    def add(part, steps, parity, arrived, after):
        shape = (len(steps), *part.shape[:1], *part.shape[2:])
        vmem = pl.BlockSpec(memory_space=pltpu.VMEM)
        given = [part] + [array for array, _ in arrived if array is not None]
        return pl.pallas_call(
            functools.partial(add_kernel, steps, parity, [place for _, place in arrived]),
            out_shape=jax.ShapeDtypeStruct(shape, jnp.bfloat16),
            in_specs=[vmem] * len(given) + [pl.BlockSpec(memory_space=pl.ANY)],
            out_specs=vmem,
            compiler_params=pltpu.CompilerParams(vmem_limit_bytes=8 << 20),
            cost_estimate=SHORT,
        )(*given, after)

    def links(step, parity):
        up = [(z, z + 1) for z in range(parity, tensor - 1, 2) if z < step]
        down = [(z + 1, z) for z in range(parity, tensor - 1, 2) if tensor - 2 - z < step]
        return up + down

    parts, arrived, sums = {}, {}, {}

    def multiply(n, after):
        parts[n] = view(head(pieces[n], head_weight, 0, cols, after))
        return parts[n]

    def send(n, steps, parity, after):
        came = [arrived.get((n, step - 1, 1 - parity), (None, None)) for step in steps]
        value = add(parts[n], steps, parity, came, after)
        moved = lax.ppermute(value, "tensor", links(steps[0], parity))
        for place, step in enumerate(steps):
            arrived[n, step, parity] = moved, place
        return value

    def sum_kernel(first, rest):
        total = first[:, chosen(lax.axis_index("tensor"))].astype(jnp.float32) if len(first.shape) == 4 else first[...]
        for ref, place in rest:
            total = total + ref[place].astype(jnp.float32)
        return total

    def ended(n, parity):
        return [arrived[n, tensor - 1, parity]] if (n, tensor - 1, parity) in arrived else []

    def finish(n, parity, after):
        given = [sums.get(n, parts[n])] + [array for array, _ in ended(n, parity)]
        places = [place for _, place in ended(n, parity)]

        def kernel(*refs):
            refs[-1][...] = sum_kernel(refs[0], zip(refs[1 : len(given)], places))

        vmem = pl.BlockSpec(memory_space=pltpu.VMEM)
        sums[n] = pl.pallas_call(
            kernel,
            out_shape=jax.ShapeDtypeStruct(parts[n].shape[:1] + parts[n].shape[2:], jnp.float32),
            in_specs=[vmem] * len(given) + [pl.BlockSpec(memory_space=pl.ANY)],
            out_specs=vmem,
            compiler_params=pltpu.CompilerParams(vmem_limit_bytes=8 << 20),
            cost_estimate=SHORT,
        )(*given, after)
        return sums[n]

    def assemble():
        *earlier, part = [sums.get(n, parts[n]) for n in parts]
        came = ended(len(parts) - 1, 0) + ended(len(parts) - 1, 1)
        given = [part] + [array for array, _ in came]
        places = [place for _, place in came]

        def kernel(*refs):
            earlier, (part, *rest), out = refs[: len(parts) - 1], refs[len(parts) - 1 : -1], refs[-1]
            turned = lax.rem(lax.axis_index("dp"), 2) if paired else 0
            for n in range(len(parts)):
                total = earlier[n][...] if n < len(earlier) else sum_kernel(part, zip(rest, places))
                total = total.reshape(sources, BLOCK, cols)
                for source in range(sources):
                    out[source ^ turned, pl.ds(n * BLOCK, BLOCK)] = total[source]

        vmem = pl.BlockSpec(memory_space=pltpu.VMEM)
        out = pl.pallas_call(
            kernel,
            out_shape=jax.ShapeDtypeStruct((sources, len(parts) * BLOCK, cols), jnp.float32),
            in_specs=[vmem] * (len(earlier) + len(given)),
            out_specs=vmem,
            compiler_params=pltpu.CompilerParams(vmem_limit_bytes=16 << 20),
            cost_estimate=SHORT,
        )(*earlier, *given)
        return out.reshape(-1, cols)

    if paired:
        along_cores(0, last)
        along_y(1, last)
        multiply(0, chips[1])
        last = send(0, (1, 2), 0, parts[0])
        along_cores(1, last)
        along_y(2, last)
        last = multiply(1, chips[2])
        last = send(1, (1, 2), 0, last)
        along_cores(2, last)
        last = multiply(2, last)
        order = [(2, (1, 2), 0), (0, (2, 3), 1), (1, (2,), 1), (1, (3,), 1), (0, (3,), 0), (2, (2,), 1), (1, (3,), 0)]
        order += [(2, (3,), 1), (1, 1), (0, 0), (0, 1), (2, (3,), 0)]
        for entry in order:
            last = finish(*entry, last) if len(entry) == 2 else send(*entry, last)
        last = finish(1, 0, last)
    else:
        for n, block in enumerate(blocks):
            pieces[n] = [lax.all_gather(block, "dp", axis=0, tiled=True)]
            last = multiply(n, last)
        for step in range(1, tensor):
            for n in range(len(blocks)):
                for parity in range(2):
                    if links(step, parity):
                        last = send(n, (step,), parity, last)

    for n in range(len(parts) - 1):
        if n not in sums:
            last = finish(n, 1, finish(n, 0, last))
    return assemble()


def solution(mesh):
    in_specs = (
        P("dp", None, "tensor"),
        P("dp", None, "tensor"),
        P("dp", None, "tensor"),
        P("dp", None, "tensor"),
        P("dp", None, "tensor"),
        P("dp"),
        P("dp"),
        P("tensor", "dp"),
    )
    out_specs = P("tensor", "dp")
    body = functools.partial(shards, mesh.shape["tensor"], mesh.shape["dp"])
    return jax.shard_map(body, mesh=mesh, in_specs=in_specs, out_specs=out_specs, check_vma=False)
```

```python
import functools

import jax
import jax.numpy as jnp
from jax import lax
from jax.experimental import pallas as pl
from jax.experimental.pallas import tpu as pltpu
from jax.sharding import PartitionSpec as P

HEAD_DIM = 128
BLOCK = 16
CHUNK = 16
LOWEST = -1e30
SHORT = pl.CostEstimate(flops=1, bytes_accessed=1, transcendentals=0)


def attend_kernel(first, rows, columns, *refs):
    all_lengths, all_accepted, queries, new_keys, new_values, key_cache, value_cache, *refs = refs
    if columns is None:
        picked, *scratch = refs
    else:
        weight, picked, held, *scratch, held_sem = refs
    lengths, accepted, q_buf, nk_buf, nv_buf, k_buf, v_buf, spread, mixed, small_sems, k_sems, v_sems = scratch
    draft, _, query_cols = q_buf.shape
    cache_len, key_cols = k_buf.shape[1:]
    groups, heads = key_cols // HEAD_DIM, query_cols // HEAD_DIM
    sharing = heads // groups
    scaling = HEAD_DIM ** (-0.5)
    own = pl.ds(first, rows)
    small = [(all_accepted, accepted), (all_lengths, lengths)]
    small += [(src.at[:, own], dst) for src, dst in ((queries, q_buf), (new_keys, nk_buf), (new_values, nv_buf))]
    small = [pltpu.make_async_copy(src, dst, small_sems.at[n]) for n, (src, dst) in enumerate(small)]
    keys, values = [
        [
            pltpu.make_async_copy(src.at[pl.ds(first + at, CHUNK)], dst.at[pl.ds(at, CHUNK)], sems.at[at // CHUNK])
            for at in range(0, rows, CHUNK)
        ]
        for src, dst, sems in ((key_cache, k_buf, k_sems), (value_cache, v_buf, v_sems))
    ]
    for copy in small:
        copy.start()
    for start in range(0, rows // CHUNK, BLOCK // CHUNK):
        for copy in keys[start : start + BLOCK // CHUNK] + values[start : start + BLOCK // CHUNK]:
            copy.start()
    if columns is not None:
        held_copy = pltpu.make_async_copy(weight.at[:, pl.ds(*columns)], held, held_sem)
        held_copy.start()
    for copy in small:
        copy.wait()
    lanes = BLOCK * heads
    nt, tn = (((1,), (1,)), ((), ())), (((0,), (0,)), ((), ()))
    lane_row = lax.broadcasted_iota(jnp.int32, (1, lanes), 1) // heads
    for block in range(0, rows, BLOCK):
        here = pl.ds(block, BLOCK)
        row = lax.broadcasted_iota(jnp.int32, (BLOCK, HEAD_DIM), 0)
        chosen = jnp.zeros((BLOCK, HEAD_DIM), jnp.int32)
        length, last = jnp.zeros((1, lanes), jnp.int32), jnp.zeros((1, lanes), jnp.int32)
        for r in range(BLOCK):
            chosen = jnp.where(row == r, accepted[first + block + r], chosen)
            last = jnp.where(lane_row == r, accepted[first + block + r], last)
            length = jnp.where(lane_row == r, lengths[first + block + r], length)
        for h in range(heads):
            cols = pl.ds(h * HEAD_DIM, HEAD_DIM)
            query = q_buf[0, here, cols].astype(jnp.float32)
            for p in range(1, draft):
                query = jnp.where(chosen == p, q_buf[p, here, cols].astype(jnp.float32), query)
            spread[:, h, :] = query
            wide = []
        for g in range(groups):
            keep = lax.broadcasted_iota(jnp.int32, spread.shape, 1) // sharing == g
            wide.append(jnp.where(keep, spread[...], 0.0).reshape(lanes, HEAD_DIM))
        query = jnp.concatenate(wide, axis=1).astype(jnp.bfloat16)

        fresh_keys = nk_buf[:, here, :].reshape(draft * BLOCK, key_cols)
        fresh_values = nv_buf[:, here, :].reshape(draft * BLOCK, key_cols)
        fresh = lax.dot_general(fresh_keys, query, nt, preferred_element_type=jnp.float32) * scaling
        slot = lax.broadcasted_iota(jnp.int32, fresh.shape, 0)
        fresh = jnp.where((slot % BLOCK == lane_row) & (slot // BLOCK <= last), fresh, LOWEST)
        past = []
        for lane in range(0, lanes, HEAD_DIM):
            part = None
            for r in range(lane // heads, (lane + HEAD_DIM) // heads):
                if r % CHUNK == 0:
                    keys[(block + r) // CHUNK].wait()
                score = lax.dot_general(
                    k_buf[block + r], query[lane : lane + HEAD_DIM], nt, preferred_element_type=jnp.float32
                )
                part = score if part is None else jnp.where(lane_row[:, lane : lane + HEAD_DIM] == r, score, part)
            past.append(part)
        past = jnp.concatenate(past, axis=1) * scaling
        past = jnp.where(lax.broadcasted_iota(jnp.int32, past.shape, 0) < length, past, LOWEST)
        peak = jnp.maximum(jnp.max(past, axis=0, keepdims=True), jnp.max(fresh, axis=0, keepdims=True))
        past, fresh = jnp.exp(past - peak), jnp.exp(fresh - peak)
        total = jnp.sum(past, axis=0, keepdims=True) + jnp.sum(fresh, axis=0, keepdims=True)
        weights = jnp.transpose(past / total)
        fresh = (fresh / total).astype(jnp.bfloat16)
        fresh = lax.dot_general(fresh, fresh_values, tn, preferred_element_type=jnp.float32)
        own_group = lax.broadcasted_iota(jnp.int32, (heads, HEAD_DIM), 0) // sharing
        for r in range(BLOCK):
            if r % CHUNK == 0:
                values[(block + r) // CHUNK].wait()
            mine = slice(r * heads, (r + 1) * heads)
            result = jnp.dot(weights[mine].astype(jnp.bfloat16), v_buf[block + r], preferred_element_type=jnp.float32)
            result = result + fresh[mine]
            kept = result[:, :HEAD_DIM]
            for g in range(1, groups):
                kept = jnp.where(own_group == g, result[:, g * HEAD_DIM : (g + 1) * HEAD_DIM], kept)
            mixed[r] = kept
        for h in range(heads):
            picked[here, pl.ds(h * HEAD_DIM, HEAD_DIM)] = mixed[:, h, :].astype(jnp.bfloat16)
    if columns is not None:
        held_copy.wait()


def attend(first, rows, arrays, after=None, weight=None, columns=None):
    draft, _, query_cols = arrays[2].shape
    _, cache_len, key_cols = arrays[5].shape
    heads = query_cols // HEAD_DIM
    vmem, anywhere = pl.BlockSpec(memory_space=pltpu.VMEM), pl.BlockSpec(memory_space=pl.ANY)
    tokens = [] if after is None else [after]
    given = [*arrays] if columns is None else [*arrays, weight]
    shapes = [jax.ShapeDtypeStruct((rows, query_cols), jnp.bfloat16)]
    if columns is not None:
        shapes.append(pltpu.VMEM((weight.shape[0], columns[1]), jnp.bfloat16))

    def kernel(*refs):
        attend_kernel(first, rows, columns, *refs[: len(given)], *refs[len(given) + len(tokens) :])

    return pl.pallas_call(
        kernel,
        out_shape=shapes,
        in_specs=[anywhere] * (len(given) + len(tokens)),
        out_specs=[vmem] * len(shapes),
        scratch_shapes=[
            pltpu.SMEM(arrays[0].shape, jnp.int32),
            pltpu.SMEM(arrays[1].shape, jnp.int32),
            pltpu.VMEM((draft, rows, query_cols), jnp.bfloat16),
            pltpu.VMEM((draft, rows, key_cols), jnp.bfloat16),
            pltpu.VMEM((draft, rows, key_cols), jnp.bfloat16),
            pltpu.VMEM((rows, cache_len, key_cols), jnp.bfloat16),
            pltpu.VMEM((rows, cache_len, key_cols), jnp.bfloat16),
            pltpu.VMEM((BLOCK, heads, HEAD_DIM), jnp.float32),
            pltpu.VMEM((BLOCK, heads, HEAD_DIM), jnp.float32),
            pltpu.SemaphoreType.DMA((5,)),
            pltpu.SemaphoreType.DMA((rows // CHUNK,)),
            pltpu.SemaphoreType.DMA((rows // CHUNK,)),
        ]
        + ([] if columns is None else [pltpu.SemaphoreType.DMA]),
        compiler_params=pltpu.CompilerParams(vmem_limit_bytes=8 << 20),
        cost_estimate=SHORT,
    )(*[pltpu.with_memory_space_constraint(a, pltpu.HBM) for a in given], *tokens)


def head_kernel(count, columns, *refs):
    pieces, refs = refs[:count], refs[count:]
    if columns is None:
        *weights, part, features = refs
    else:
        *weights, weight, part, held, features, held_sem = refs
        held_copy = pltpu.make_async_copy(weight.at[:, pl.ds(*columns)], held, held_sem)
        held_copy.start()
        weights.append(held)
    at = 0
    for piece in pieces:
        features[pl.ds(at, piece.shape[0]), :] = piece[...]
        at += piece.shape[0]
    at = 0
    for n, weight in enumerate(weights):
        if columns is not None and n == len(weights) - 1:
            held_copy.wait()
        tile = min(512, weight.shape[1])
        for start in range(0, weight.shape[1], tile):
            product = jnp.dot(features[...], weight[:, pl.ds(start, tile)], preferred_element_type=jnp.float32)
            part[:, pl.ds(at + start, tile)] = product.astype(jnp.bfloat16)
        at += weight.shape[1]


def head(pieces, weights, after, weight=None, columns=None):
    depth = weights[0].shape[0]
    rows = sum(piece.shape[0] for piece in pieces)
    cols = sum(weight.shape[1] for weight in weights) + (0 if columns is None else columns[1])
    vmem, anywhere = pl.BlockSpec(memory_space=pltpu.VMEM), pl.BlockSpec(memory_space=pl.ANY)
    given = [*pieces, *[pltpu.with_memory_space_constraint(weight, pltpu.VMEM) for weight in weights]]
    specs = [vmem] * len(given)
    shapes = [jax.ShapeDtypeStruct((rows, cols), jnp.bfloat16)]
    if columns is not None:
        given.append(pltpu.with_memory_space_constraint(weight, pltpu.HBM))
        specs.append(anywhere)
        shapes.append(pltpu.VMEM((depth, columns[1]), jnp.bfloat16))

    def kernel(*refs):
        head_kernel(len(pieces), columns, *refs[: len(given)], *refs[len(given) + 1 :])

    return pl.pallas_call(
        kernel,
        out_shape=shapes,
        in_specs=[*specs, anywhere],
        out_specs=[vmem] * len(shapes),
        scratch_shapes=[pltpu.VMEM((rows, depth), jnp.bfloat16)]
        + ([] if columns is None else [pltpu.SemaphoreType.DMA]),
        compiler_params=pltpu.CompilerParams(vmem_limit_bytes=8 << 20),
        cost_estimate=SHORT,
    )(*given, after)


def swap(array, dp, bits):
    return lax.ppermute(array, "dp", [(i, i ^ bits) for i in range(dp)])


def behind(array, other):
    return lax.optimization_barrier((array, other))[0]


def shards(
    tensor, dp, queries, new_keys, new_values, key_cache, value_cache, cache_lengths, accepted, head_weight
):
    rows_dev = queries.shape[0]
    queries, new_keys, new_values = [jnp.transpose(a, (1, 0, 2)) for a in (queries, new_keys, new_values)]
    arrays = (cache_lengths, accepted, queries, new_keys, new_values, key_cache, value_cache)
    sources = dp // tensor
    paired = dp == 8 and tensor == 4
    cols = head_weight.shape[1]

    groups = rows_dev // BLOCK
    share = cols // (groups + 1)
    first, weight = attend(0, BLOCK, arrays, None, head_weight, (0, share))
    blocks, weights, chips, pieces, last = [first], [weight], {}, {}, first
    for n in range(1, groups):
        if paired:
            chips[n - 1] = swap(blocks[n - 1], dp, 2)
        block, weight = attend(n * BLOCK, BLOCK, arrays, last, head_weight, (n * share, share))
        blocks.append(block)
        weights.append(weight)
        last = block
        if paired and n == 1:
            last = chips[0] = jnp.concatenate([first, behind(chips[0], block)])
    if paired:
        chips[groups - 1] = swap(blocks[-1], dp, 2)

    def along_y(n, after):
        chips[n] = jnp.concatenate([blocks[n], behind(chips[n], after)])

    def along_cores(n, after):
        both = jnp.concatenate([chips[n], behind(swap(chips[n], dp, 4), after)])
        pieces[n] = [both, swap(both, dp, 1)]

    def view(part):
        if paired:
            return part.reshape(2, tensor, -1, part.shape[-1])
        return part.reshape(1, tensor, -1, part.shape[-1])

    def chosen(shard):
        return shard ^ (lax.axis_index("dp") // 2) if paired else shard

    def add_kernel(parity, sources, *refs):
        *refs, sent = refs
        z = lax.axis_index("tensor")
        for n, (part, step, arrived, place) in enumerate(sources):
            shard = jnp.where(lax.rem(z, 2) == parity, tensor - step + z, step - tensor + z)
            at = chosen(jnp.clip(shard, 0, tensor - 1))
            if arrived is None:
                sent[n] = refs[part][:, at]
            else:
                total = refs[part][:, at].astype(jnp.float32) + refs[arrived][place].astype(jnp.float32)
                sent[n] = total.astype(jnp.bfloat16)

    def add(terms, parity, after):
        part = terms[0][0]
        shape = (len(terms), *part.shape[:1], *part.shape[2:])
        vmem = pl.BlockSpec(memory_space=pltpu.VMEM)
        given, sources = [], []
        for part, step, array, place in terms:
            sources.append((len(given), step, None if array is None else len(given) + 1, place))
            given += [part] if array is None else [part, array]
        return pl.pallas_call(
            lambda *refs: add_kernel(parity, sources, *refs[: len(given)], refs[-1]),
            out_shape=jax.ShapeDtypeStruct(shape, jnp.bfloat16),
            in_specs=[vmem] * len(given) + [pl.BlockSpec(memory_space=pl.ANY)],
            out_specs=vmem,
            compiler_params=pltpu.CompilerParams(vmem_limit_bytes=8 << 20),
            cost_estimate=SHORT,
        )(*given, after)

    def links(step, parity):
        up = [(z, z + 1) for z in range(parity, tensor - 1, 2) if z < step]
        down = [(z + 1, z) for z in range(parity, tensor - 1, 2) if tensor - 2 - z < step]
        return up + down

    parts, arrived, sums = {}, {}, {}

    def multiply(n, after):
        if n == 0:
            part, weight = head(pieces[n], weights, after, head_weight, (groups * share, cols - groups * share))
            weights.append(weight)
        else:
            (part,) = head(pieces[n], weights, after)
        parts[n] = view(part)
        return parts[n]

    def send(entries, parity, after):
        terms = [(parts[n], step, *arrived.get((n, step - 1, 1 - parity), (None, None))) for n, step in entries]
        value = add(terms, parity, after)
        moved = lax.ppermute(value, "tensor", links(entries[0][1], parity))
        for place, (n, step) in enumerate(entries):
            arrived[n, step, parity] = moved, place
        return value

    def sum_kernel(first, rest):
        total = first[:, chosen(lax.axis_index("tensor"))].astype(jnp.float32) if len(first.shape) == 4 else first[...]
        for ref, place in rest:
            total = total + ref[place].astype(jnp.float32)
        return total

    def ended(n, parity):
        return [arrived[n, tensor - 1, parity]] if (n, tensor - 1, parity) in arrived else []

    def finish(n, parity, after):
        given = [sums.get(n, parts[n])] + [array for array, _ in ended(n, parity)]
        places = [place for _, place in ended(n, parity)]

        def kernel(*refs):
            refs[-1][...] = sum_kernel(refs[0], zip(refs[1 : len(given)], places))

        vmem = pl.BlockSpec(memory_space=pltpu.VMEM)
        sums[n] = pl.pallas_call(
            kernel,
            out_shape=jax.ShapeDtypeStruct(parts[n].shape[:1] + parts[n].shape[2:], jnp.float32),
            in_specs=[vmem] * len(given) + [pl.BlockSpec(memory_space=pl.ANY)],
            out_specs=vmem,
            compiler_params=pltpu.CompilerParams(vmem_limit_bytes=8 << 20),
            cost_estimate=SHORT,
        )(*given, after)
        return sums[n]

    def assemble():
        *earlier, part = [sums.get(n, parts[n]) for n in parts]
        came = ended(len(parts) - 1, 0) + ended(len(parts) - 1, 1)
        given = [part] + [array for array, _ in came]
        places = [place for _, place in came]

        def kernel(*refs):
            earlier, (part, *rest), out = refs[: len(parts) - 1], refs[len(parts) - 1 : -1], refs[-1]
            turned = lax.rem(lax.axis_index("dp"), 2) if paired else 0
            for n in range(len(parts)):
                total = earlier[n][...] if n < len(earlier) else sum_kernel(part, zip(rest, places))
                total = total.reshape(sources, BLOCK, cols)
                for source in range(sources):
                    out[source ^ turned, pl.ds(n * BLOCK, BLOCK)] = total[source]

        vmem = pl.BlockSpec(memory_space=pltpu.VMEM)
        out = pl.pallas_call(
            kernel,
            out_shape=jax.ShapeDtypeStruct((sources, len(parts) * BLOCK, cols), jnp.float32),
            in_specs=[vmem] * (len(earlier) + len(given)),
            out_specs=vmem,
            compiler_params=pltpu.CompilerParams(vmem_limit_bytes=16 << 20),
            cost_estimate=SHORT,
        )(*earlier, *given)
        return out.reshape(-1, cols)

    if paired:
        along_cores(0, last)
        multiply(0, pieces[0][1])
        last = send([(0, 1), (0, 2)], 0, parts[0])
        along_y(1, last)
        along_cores(1, last)
        along_y(2, last)
        last = multiply(1, last)
        last = send([(1, 1), (1, 2)], 0, last)
        last = send([(0, 2), (0, 3)], 1, last)
        along_cores(2, last)
        last = multiply(2, last)
        last = send([(2, 1), (2, 2)], 0, last)
        last = send([(1, 2)], 1, last)
        last = send([(1, 3)], 1, last)
        last = send([(0, 3), (1, 3)], 0, last)
        last = send([(2, 2)], 1, last)
        last = send([(2, 3)], 1, last)
        last = finish(0, 1, last)
        last = finish(1, 1, last)
        last = send([(2, 3)], 0, last)
        last = finish(0, 0, last)
        last = finish(1, 0, last)
    else:
        for n, block in enumerate(blocks):
            pieces[n] = [lax.all_gather(block, "dp", axis=0, tiled=True)]
            last = multiply(n, last)
        for step in range(1, tensor):
            for n in range(len(blocks)):
                for parity in range(2):
                    if links(step, parity):
                        last = send([(n, step)], parity, last)

    for n in range(len(parts) - 1):
        if n not in sums:
            last = finish(n, 1, finish(n, 0, last))
    return assemble()


def solution(mesh):
    in_specs = (
        P("dp", None, "tensor"),
        P("dp", None, "tensor"),
        P("dp", None, "tensor"),
        P("dp", None, "tensor"),
        P("dp", None, "tensor"),
        P("dp"),
        P("dp"),
        P("tensor", "dp"),
    )
    out_specs = P("tensor", "dp")
    body = functools.partial(shards, mesh.shape["tensor"], mesh.shape["dp"])
    return jax.shard_map(body, mesh=mesh, in_specs=in_specs, out_specs=out_specs, check_vma=False)
```

```python
import functools

import jax
import jax.numpy as jnp
from jax import lax
from jax.experimental import pallas as pl
from jax.experimental.pallas import tpu as pltpu
from jax.sharding import PartitionSpec as P

HEAD_DIM = 128
BLOCK = 16
CHUNK = 16
LOWEST = -1e30
SHORT = pl.CostEstimate(flops=1, bytes_accessed=1, transcendentals=0)


ORDER = [
    ("cores", 0),
    ("below", 1),
    ("ends", 0),
    ("send", [(0, 1), (0, 2)], 0),
    ("between", 0),
    ("beside", 2),
    ("cores", 1),
    ("below", 2),
    ("head", 1),
    ("send", [(1, 1), (1, 2)], 0),
    ("send", [(0, 2), (0, 3)], 1),
    ("cores", 2),
    ("head", 2),
    ("send", [(2, 1)], 0),
    ("send", [(2, 2)], 0),
    ("send", [(1, 2)], 1),
    ("send", [(0, 3)], 0),
    ("send", [(2, 2)], 1),
    ("send", [(1, 3)], 0),
    ("send", [(1, 3)], 1),
    ("send", [(2, 3)], 1),
    ("finish", 0, 1),
    ("finish", 0, 0),
    ("send", [(2, 3)], 0),
    ("finish", 1, 1),
    ("finish", 1, 0),
]


def attend_kernel(first, rows, columns, *refs):
    all_lengths, all_accepted, queries, new_keys, new_values, key_cache, value_cache, *refs = refs
    if columns is None:
        picked, *scratch = refs
    else:
        weight, picked, held, *scratch, held_sem = refs
    lengths, accepted, q_buf, nk_buf, nv_buf, k_buf, v_buf, spread, mixed, small_sems, k_sems, v_sems = scratch
    draft, _, query_cols = q_buf.shape
    cache_len, key_cols = k_buf.shape[1:]
    groups, heads = key_cols // HEAD_DIM, query_cols // HEAD_DIM
    sharing = heads // groups
    scaling = HEAD_DIM ** (-0.5)
    own = pl.ds(first, rows)
    small = [(all_accepted, accepted), (all_lengths, lengths)]
    small += [(src.at[:, own], dst) for src, dst in ((queries, q_buf), (new_keys, nk_buf), (new_values, nv_buf))]
    small = [pltpu.make_async_copy(src, dst, small_sems.at[n]) for n, (src, dst) in enumerate(small)]
    keys, values = [
        [
            pltpu.make_async_copy(src.at[pl.ds(first + at, CHUNK)], dst.at[pl.ds(at, CHUNK)], sems.at[at // CHUNK])
            for at in range(0, rows, CHUNK)
        ]
        for src, dst, sems in ((key_cache, k_buf, k_sems), (value_cache, v_buf, v_sems))
    ]
    for copy in small:
        copy.start()
    for start in range(0, rows // CHUNK, BLOCK // CHUNK):
        for copy in keys[start : start + BLOCK // CHUNK] + values[start : start + BLOCK // CHUNK]:
            copy.start()
    if columns is not None:
        held_copy = pltpu.make_async_copy(weight.at[:, pl.ds(*columns)], held, held_sem)
        held_copy.start()
    for copy in small:
        copy.wait()
    lanes = BLOCK * heads
    nt, tn = (((1,), (1,)), ((), ())), (((0,), (0,)), ((), ()))
    lane_row = lax.broadcasted_iota(jnp.int32, (1, lanes), 1) // heads
    for block in range(0, rows, BLOCK):
        here = pl.ds(block, BLOCK)
        row = lax.broadcasted_iota(jnp.int32, (BLOCK, HEAD_DIM), 0)
        chosen = jnp.zeros((BLOCK, HEAD_DIM), jnp.int32)
        length, last = jnp.zeros((1, lanes), jnp.int32), jnp.zeros((1, lanes), jnp.int32)
        for r in range(BLOCK):
            chosen = jnp.where(row == r, accepted[first + block + r], chosen)
            last = jnp.where(lane_row == r, accepted[first + block + r], last)
            length = jnp.where(lane_row == r, lengths[first + block + r], length)
        for h in range(heads):
            cols = pl.ds(h * HEAD_DIM, HEAD_DIM)
            query = q_buf[0, here, cols].astype(jnp.float32)
            for p in range(1, draft):
                query = jnp.where(chosen == p, q_buf[p, here, cols].astype(jnp.float32), query)
            spread[:, h, :] = query
            wide = []
        for g in range(groups):
            keep = lax.broadcasted_iota(jnp.int32, spread.shape, 1) // sharing == g
            wide.append(jnp.where(keep, spread[...], 0.0).reshape(lanes, HEAD_DIM))
        query = jnp.concatenate(wide, axis=1).astype(jnp.bfloat16)

        fresh_keys = nk_buf[:, here, :].reshape(draft * BLOCK, key_cols)
        fresh_values = nv_buf[:, here, :].reshape(draft * BLOCK, key_cols)
        fresh = lax.dot_general(fresh_keys, query, nt, preferred_element_type=jnp.float32) * scaling
        slot = lax.broadcasted_iota(jnp.int32, fresh.shape, 0)
        fresh = jnp.where((slot % BLOCK == lane_row) & (slot // BLOCK <= last), fresh, LOWEST)
        past = []
        for lane in range(0, lanes, HEAD_DIM):
            part = None
            for r in range(lane // heads, (lane + HEAD_DIM) // heads):
                if r % CHUNK == 0:
                    keys[(block + r) // CHUNK].wait()
                score = lax.dot_general(
                    k_buf[block + r], query[lane : lane + HEAD_DIM], nt, preferred_element_type=jnp.float32
                )
                part = score if part is None else jnp.where(lane_row[:, lane : lane + HEAD_DIM] == r, score, part)
            past.append(part)
        past = jnp.concatenate(past, axis=1) * scaling
        past = jnp.where(lax.broadcasted_iota(jnp.int32, past.shape, 0) < length, past, LOWEST)
        peak = jnp.maximum(jnp.max(past, axis=0, keepdims=True), jnp.max(fresh, axis=0, keepdims=True))
        past, fresh = jnp.exp(past - peak), jnp.exp(fresh - peak)
        total = jnp.sum(past, axis=0, keepdims=True) + jnp.sum(fresh, axis=0, keepdims=True)
        weights = jnp.transpose(past / total)
        fresh = (fresh / total).astype(jnp.bfloat16)
        fresh = lax.dot_general(fresh, fresh_values, tn, preferred_element_type=jnp.float32)
        own_group = lax.broadcasted_iota(jnp.int32, (heads, HEAD_DIM), 0) // sharing
        for r in range(BLOCK):
            if r % CHUNK == 0:
                values[(block + r) // CHUNK].wait()
            mine = slice(r * heads, (r + 1) * heads)
            result = jnp.dot(weights[mine].astype(jnp.bfloat16), v_buf[block + r], preferred_element_type=jnp.float32)
            result = result + fresh[mine]
            kept = result[:, :HEAD_DIM]
            for g in range(1, groups):
                kept = jnp.where(own_group == g, result[:, g * HEAD_DIM : (g + 1) * HEAD_DIM], kept)
            mixed[r] = kept
        for h in range(heads):
            picked[here, pl.ds(h * HEAD_DIM, HEAD_DIM)] = mixed[:, h, :].astype(jnp.bfloat16)
    if columns is not None:
        held_copy.wait()


def attend(first, rows, arrays, after=None, weight=None, columns=None):
    draft, _, query_cols = arrays[2].shape
    _, cache_len, key_cols = arrays[5].shape
    heads = query_cols // HEAD_DIM
    vmem, anywhere = pl.BlockSpec(memory_space=pltpu.VMEM), pl.BlockSpec(memory_space=pl.ANY)
    tokens = [] if after is None else [after]
    given = [*arrays] if columns is None else [*arrays, weight]
    shapes = [jax.ShapeDtypeStruct((rows, query_cols), jnp.bfloat16)]
    if columns is not None:
        shapes.append(pltpu.VMEM((weight.shape[0], columns[1]), jnp.bfloat16))

    def kernel(*refs):
        attend_kernel(first, rows, columns, *refs[: len(given)], *refs[len(given) + len(tokens) :])

    return pl.pallas_call(
        kernel,
        out_shape=shapes,
        in_specs=[anywhere] * (len(given) + len(tokens)),
        out_specs=[vmem] * len(shapes),
        scratch_shapes=[
            pltpu.SMEM(arrays[0].shape, jnp.int32),
            pltpu.SMEM(arrays[1].shape, jnp.int32),
            pltpu.VMEM((draft, rows, query_cols), jnp.bfloat16),
            pltpu.VMEM((draft, rows, key_cols), jnp.bfloat16),
            pltpu.VMEM((draft, rows, key_cols), jnp.bfloat16),
            pltpu.VMEM((rows, cache_len, key_cols), jnp.bfloat16),
            pltpu.VMEM((rows, cache_len, key_cols), jnp.bfloat16),
            pltpu.VMEM((BLOCK, heads, HEAD_DIM), jnp.float32),
            pltpu.VMEM((BLOCK, heads, HEAD_DIM), jnp.float32),
            pltpu.SemaphoreType.DMA((5,)),
            pltpu.SemaphoreType.DMA((rows // CHUNK,)),
            pltpu.SemaphoreType.DMA((rows // CHUNK,)),
        ]
        + ([] if columns is None else [pltpu.SemaphoreType.DMA]),
        compiler_params=pltpu.CompilerParams(vmem_limit_bytes=8 << 20),
        cost_estimate=SHORT,
    )(*[pltpu.with_memory_space_constraint(a, pltpu.HBM) for a in given], *tokens)


def multiply_pieces(pieces, weights, part, features):
    at = 0
    for piece in pieces:
        features[pl.ds(at, piece.shape[0]), :] = piece[...]
        at += piece.shape[0]
    at = 0
    for weight in weights:
        for start in range(0, weight.shape[1], 512):
            tile = min(512, weight.shape[1] - start)
            product = jnp.dot(features[...], weight[:, pl.ds(start, tile)], preferred_element_type=jnp.float32)
            part[:, pl.ds(at + start, tile)] = product.astype(jnp.bfloat16)
        at += weight.shape[1]


def head(pieces, weights, after, works=None, otherwise=None):
    depth = weights[0].shape[0]
    rows = sum(piece.shape[0] for piece in pieces)
    cols = sum(weight.shape[1] for weight in weights)
    vmem, anywhere = pl.BlockSpec(memory_space=pltpu.VMEM), pl.BlockSpec(memory_space=pl.ANY)
    given = [*pieces, *[pltpu.with_memory_space_constraint(weight, pltpu.VMEM) for weight in weights]]
    given += [] if otherwise is None else [otherwise]

    def kernel(*refs):
        sides = refs[len(pieces) : len(pieces) + len(weights)]
        part, features = refs[-2:]
        if works is None:
            multiply_pieces(refs[: len(pieces)], sides, part, features)
        else:

            @pl.when(works())
            def _():
                multiply_pieces(refs[: len(pieces)], sides, part, features)

            if otherwise is not None:

                @pl.when(jnp.logical_not(works()))
                def _():
                    part[...] = refs[len(given) - 1][...]

    return pl.pallas_call(
        kernel,
        out_shape=jax.ShapeDtypeStruct((rows, cols), jnp.bfloat16),
        in_specs=[vmem] * len(given) + [anywhere],
        out_specs=vmem,
        scratch_shapes=[pltpu.VMEM((rows, depth), jnp.bfloat16)],
        compiler_params=pltpu.CompilerParams(vmem_limit_bytes=8 << 20),
        cost_estimate=SHORT,
    )(*given, after)


def swap(array, dp, bits):
    return lax.ppermute(array, "dp", [(i, i ^ bits) for i in range(dp)])


def behind(array, other):
    return lax.optimization_barrier((array, other))[0]


def shards(
    tensor, dp, queries, new_keys, new_values, key_cache, value_cache, cache_lengths, accepted, head_weight
):
    rows_dev = queries.shape[0]
    queries, new_keys, new_values = [jnp.transpose(a, (1, 0, 2)) for a in (queries, new_keys, new_values)]
    arrays = (cache_lengths, accepted, queries, new_keys, new_values, key_cache, value_cache)
    sources = dp // tensor
    paired = dp == 8 and tensor == 4
    cols = head_weight.shape[1]

    groups = rows_dev // BLOCK
    unit = cols // 8
    columns = [(0, 2 * unit), (2 * unit, 3 * unit), (5 * unit, 3 * unit)]
    first, weight = attend(0, BLOCK, arrays, None, head_weight, columns[0])
    blocks, weights, chips, pieces, last = [first], [weight], {}, {}, first
    for n in range(1, groups):
        if paired:
            chips[n - 1] = swap(blocks[n - 1], dp, 2)
        block, weight = attend(n * BLOCK, BLOCK, arrays, last, head_weight, columns[n])
        blocks.append(block)
        weights.append(weight)
        last = block
        if paired and n == 1:
            last = chips[0] = jnp.concatenate([first, behind(chips[0], block)])

    def along_y(n, after):
        chips[n] = jnp.concatenate([blocks[n], behind(chips[n], after)])

    def along_cores(n, after):
        both = jnp.concatenate([chips[n], behind(swap(chips[n], dp, 4), after)])
        pieces[n] = [both, swap(both, dp, 1)]

    def view(part):
        if paired:
            return part.reshape(2, tensor, -1, part.shape[-1])
        return part.reshape(1, tensor, -1, part.shape[-1])

    def chosen(shard):
        return shard ^ (lax.axis_index("dp") // 2) if paired else shard

    def add_kernel(parity, sources, *refs):
        *refs, sent = refs
        z = lax.axis_index("tensor")
        for n, (part, step, arrived, place) in enumerate(sources):
            shard = jnp.where(lax.rem(z, 2) == parity, tensor - step + z, step - tensor + z)
            at = chosen(jnp.clip(shard, 0, tensor - 1))
            if arrived is None:
                sent[n] = refs[part][:, at]
            else:
                total = refs[part][:, at].astype(jnp.float32) + refs[arrived][place].astype(jnp.float32)
                sent[n] = total.astype(jnp.bfloat16)

    def add(terms, parity, after):
        part = terms[0][0]
        shape = (len(terms), *part.shape[:1], *part.shape[2:])
        vmem = pl.BlockSpec(memory_space=pltpu.VMEM)
        given, sources = [], []
        for part, step, array, place in terms:
            sources.append((len(given), step, None if array is None else len(given) + 1, place))
            given += [part] if array is None else [part, array]
        return pl.pallas_call(
            lambda *refs: add_kernel(parity, sources, *refs[: len(given)], refs[-1]),
            out_shape=jax.ShapeDtypeStruct(shape, jnp.bfloat16),
            in_specs=[vmem] * len(given) + [pl.BlockSpec(memory_space=pl.ANY)],
            out_specs=vmem,
            compiler_params=pltpu.CompilerParams(vmem_limit_bytes=8 << 20),
            cost_estimate=SHORT,
        )(*given, after)

    def links(step, parity):
        up = [(z, z + 1) for z in range(parity, tensor - 1, 2) if z < step]
        down = [(z + 1, z) for z in range(parity, tensor - 1, 2) if tensor - 2 - z < step]
        return up + down

    parts, arrived, sums = {}, {}, {}

    def at_end():
        return (lax.axis_index("tensor") == 0) | (lax.axis_index("tensor") == tensor - 1)

    def multiply(n, after, works=None, otherwise=None):
        parts[n] = view(head(pieces[n], weights, after, works, otherwise))
        return parts[n]

    def send(entries, parity, after):
        terms = [(parts[n], step, *arrived.get((n, step - 1, 1 - parity), (None, None))) for n, step in entries]
        value = add(terms, parity, after)
        moved = lax.ppermute(value, "tensor", links(entries[0][1], parity))
        for place, (n, step) in enumerate(entries):
            arrived[n, step, parity] = moved, place
        return value

    def sum_kernel(first, rest):
        total = first[:, chosen(lax.axis_index("tensor"))].astype(jnp.float32) if len(first.shape) == 4 else first[...]
        for ref, place in rest:
            total = total + ref[place].astype(jnp.float32)
        return total

    def ended(n, parity):
        return [arrived[n, tensor - 1, parity]] if (n, tensor - 1, parity) in arrived else []

    def finish(n, parity, after):
        given = [sums.get(n, parts[n])] + [array for array, _ in ended(n, parity)]
        places = [place for _, place in ended(n, parity)]

        def kernel(*refs):
            refs[-1][...] = sum_kernel(refs[0], zip(refs[1 : len(given)], places))

        vmem = pl.BlockSpec(memory_space=pltpu.VMEM)
        sums[n] = pl.pallas_call(
            kernel,
            out_shape=jax.ShapeDtypeStruct(parts[n].shape[:1] + parts[n].shape[2:], jnp.float32),
            in_specs=[vmem] * len(given) + [pl.BlockSpec(memory_space=pl.ANY)],
            out_specs=vmem,
            compiler_params=pltpu.CompilerParams(vmem_limit_bytes=8 << 20),
            cost_estimate=SHORT,
        )(*given, after)
        return sums[n]

    def assemble():
        *earlier, part = [sums.get(n, parts[n]) for n in parts]
        came = ended(len(parts) - 1, 0) + ended(len(parts) - 1, 1)
        given = [part] + [array for array, _ in came]
        places = [place for _, place in came]

        def kernel(*refs):
            earlier, (part, *rest), out = refs[: len(parts) - 1], refs[len(parts) - 1 : -1], refs[-1]
            turned = lax.rem(lax.axis_index("dp"), 2) if paired else 0
            for n in range(len(parts)):
                total = earlier[n][...] if n < len(earlier) else sum_kernel(part, zip(rest, places))
                total = total.reshape(sources, BLOCK, cols)
                for source in range(sources):
                    out[source ^ turned, pl.ds(n * BLOCK, BLOCK)] = total[source]

        vmem = pl.BlockSpec(memory_space=pltpu.VMEM)
        out = pl.pallas_call(
            kernel,
            out_shape=jax.ShapeDtypeStruct((sources, len(parts) * BLOCK, cols), jnp.float32),
            in_specs=[vmem] * (len(earlier) + len(given)),
            out_specs=vmem,
            compiler_params=pltpu.CompilerParams(vmem_limit_bytes=16 << 20),
            cost_estimate=SHORT,
        )(*earlier, *given)
        return out.reshape(-1, cols)

    if paired:
        for step, *what in ORDER:
            if step == "beside":
                chips[what[0]] = swap(behind(blocks[what[0]], last), dp, 2)
            elif step == "below":
                along_y(what[0], last)
            elif step == "cores":
                along_cores(what[0], last)
            elif step == "ends":
                last = multiply(what[0], last, at_end)
            elif step == "between":
                last = multiply(what[0], last, lambda: ~at_end(), parts[what[0]].reshape(-1, cols))
            elif step == "head":
                last = multiply(what[0], last)
            elif step == "send":
                last = send(*what, last)
            else:
                last = finish(*what, last)
    else:
        for n, block in enumerate(blocks):
            pieces[n] = [lax.all_gather(block, "dp", axis=0, tiled=True)]
            last = multiply(n, last)
        for step in range(1, tensor):
            for n in range(len(blocks)):
                for parity in range(2):
                    if links(step, parity):
                        last = send([(n, step)], parity, last)

    for n in range(len(parts) - 1):
        if n not in sums:
            last = finish(n, 1, finish(n, 0, last))
    return assemble()


def solution(mesh):
    in_specs = (
        P("dp", None, "tensor"),
        P("dp", None, "tensor"),
        P("dp", None, "tensor"),
        P("dp", None, "tensor"),
        P("dp", None, "tensor"),
        P("dp"),
        P("dp"),
        P("tensor", "dp"),
    )
    out_specs = P("tensor", "dp")
    body = functools.partial(shards, mesh.shape["tensor"], mesh.shape["dp"])
    return jax.shard_map(body, mesh=mesh, in_specs=in_specs, out_specs=out_specs, check_vma=False)
```

```python
import functools

import jax
import jax.numpy as jnp
from jax import lax
from jax.experimental import pallas as pl
from jax.experimental.pallas import tpu as pltpu
from jax.sharding import PartitionSpec as P

HEAD_DIM = 128
BLOCK = 16
CHUNK = 16
LOWEST = -1e30
SHORT = pl.CostEstimate(flops=1, bytes_accessed=1, transcendentals=0)


ORDER = [
    ("cores", 0),
    ("below", 1),
    ("ends", 0),
    ("send", [(0, 1), (0, 2)], 0),
    ("between", 0),
    ("beside", 2),
    ("cores", 1),
    ("below", 2),
    ("head", 1),
    ("send", [(1, 1), (1, 2)], 0),
    ("send", [(0, 2), (0, 3)], 1),
    ("cores", 2),
    ("head", 2),
    ("send", [(2, 1)], 0),
    ("send", [(2, 2)], 0),
    ("send", [(1, 2)], 1),
    ("send", [(0, 3)], 0),
    ("send", [(2, 2)], 1),
    ("send", [(2, 3)], 1),
    ("send", [(1, 3)], 0),
    ("send", [(1, 3)], 1),
    ("finish", 0, 1),
    ("finish", 0, 0),
    ("send", [(2, 3)], 0),
    ("finish", 1, 1),
    ("finish", 1, 0),
]


def attend_kernel(first, rows, columns, *refs):
    all_lengths, all_accepted, queries, new_keys, new_values, key_cache, value_cache, *refs = refs
    if columns is None:
        picked, *scratch = refs
    else:
        weight, picked, held, *scratch, held_sem = refs
    lengths, accepted, q_buf, nk_buf, nv_buf, k_buf, v_buf, spread, mixed, small_sems, k_sems, v_sems = scratch
    draft, _, query_cols = q_buf.shape
    cache_len, key_cols = k_buf.shape[1:]
    groups, heads = key_cols // HEAD_DIM, query_cols // HEAD_DIM
    sharing = heads // groups
    scaling = HEAD_DIM ** (-0.5)
    own = pl.ds(first, rows)
    small = [(all_accepted, accepted), (all_lengths, lengths)]
    small += [(src.at[:, own], dst) for src, dst in ((queries, q_buf), (new_keys, nk_buf), (new_values, nv_buf))]
    small = [pltpu.make_async_copy(src, dst, small_sems.at[n]) for n, (src, dst) in enumerate(small)]
    keys, values = [
        [
            pltpu.make_async_copy(src.at[pl.ds(first + at, CHUNK)], dst.at[pl.ds(at, CHUNK)], sems.at[at // CHUNK])
            for at in range(0, rows, CHUNK)
        ]
        for src, dst, sems in ((key_cache, k_buf, k_sems), (value_cache, v_buf, v_sems))
    ]
    for copy in small:
        copy.start()
    for start in range(0, rows // CHUNK, BLOCK // CHUNK):
        for copy in keys[start : start + BLOCK // CHUNK] + values[start : start + BLOCK // CHUNK]:
            copy.start()
    if columns is not None:
        held_copy = pltpu.make_async_copy(weight.at[:, pl.ds(*columns)], held, held_sem)
        held_copy.start()
    for copy in small:
        copy.wait()
    lanes = BLOCK * heads
    nt, tn = (((1,), (1,)), ((), ())), (((0,), (0,)), ((), ()))
    lane_row = lax.broadcasted_iota(jnp.int32, (1, lanes), 1) // heads
    for block in range(0, rows, BLOCK):
        here = pl.ds(block, BLOCK)
        row = lax.broadcasted_iota(jnp.int32, (BLOCK, HEAD_DIM), 0)
        chosen = jnp.zeros((BLOCK, HEAD_DIM), jnp.int32)
        length, last = jnp.zeros((1, lanes), jnp.int32), jnp.zeros((1, lanes), jnp.int32)
        for r in range(BLOCK):
            chosen = jnp.where(row == r, accepted[first + block + r], chosen)
            last = jnp.where(lane_row == r, accepted[first + block + r], last)
            length = jnp.where(lane_row == r, lengths[first + block + r], length)
        for h in range(heads):
            cols = pl.ds(h * HEAD_DIM, HEAD_DIM)
            query = q_buf[0, here, cols].astype(jnp.float32)
            for p in range(1, draft):
                query = jnp.where(chosen == p, q_buf[p, here, cols].astype(jnp.float32), query)
            spread[:, h, :] = query
            wide = []
        for g in range(groups):
            keep = lax.broadcasted_iota(jnp.int32, spread.shape, 1) // sharing == g
            wide.append(jnp.where(keep, spread[...], 0.0).reshape(lanes, HEAD_DIM))
        query = jnp.concatenate(wide, axis=1).astype(jnp.bfloat16)

        fresh_keys = nk_buf[:, here, :].reshape(draft * BLOCK, key_cols)
        fresh_values = nv_buf[:, here, :].reshape(draft * BLOCK, key_cols)
        fresh = lax.dot_general(fresh_keys, query, nt, preferred_element_type=jnp.float32) * scaling
        slot = lax.broadcasted_iota(jnp.int32, fresh.shape, 0)
        fresh = jnp.where((slot % BLOCK == lane_row) & (slot // BLOCK <= last), fresh, LOWEST)
        past = []
        for lane in range(0, lanes, HEAD_DIM):
            part = None
            for r in range(lane // heads, (lane + HEAD_DIM) // heads):
                if r % CHUNK == 0:
                    keys[(block + r) // CHUNK].wait()
                score = lax.dot_general(
                    k_buf[block + r], query[lane : lane + HEAD_DIM], nt, preferred_element_type=jnp.float32
                )
                part = score if part is None else jnp.where(lane_row[:, lane : lane + HEAD_DIM] == r, score, part)
            past.append(part)
        past = jnp.concatenate(past, axis=1) * scaling
        past = jnp.where(lax.broadcasted_iota(jnp.int32, past.shape, 0) < length, past, LOWEST)
        peak = jnp.maximum(jnp.max(past, axis=0, keepdims=True), jnp.max(fresh, axis=0, keepdims=True))
        past, fresh = jnp.exp(past - peak), jnp.exp(fresh - peak)
        total = jnp.sum(past, axis=0, keepdims=True) + jnp.sum(fresh, axis=0, keepdims=True)
        weights = jnp.transpose(past / total)
        fresh = (fresh / total).astype(jnp.bfloat16)
        fresh = lax.dot_general(fresh, fresh_values, tn, preferred_element_type=jnp.float32)
        own_group = lax.broadcasted_iota(jnp.int32, (heads, HEAD_DIM), 0) // sharing
        for r in range(BLOCK):
            if r % CHUNK == 0:
                values[(block + r) // CHUNK].wait()
            mine = slice(r * heads, (r + 1) * heads)
            result = jnp.dot(weights[mine].astype(jnp.bfloat16), v_buf[block + r], preferred_element_type=jnp.float32)
            result = result + fresh[mine]
            kept = result[:, :HEAD_DIM]
            for g in range(1, groups):
                kept = jnp.where(own_group == g, result[:, g * HEAD_DIM : (g + 1) * HEAD_DIM], kept)
            mixed[r] = kept
        for h in range(heads):
            picked[here, pl.ds(h * HEAD_DIM, HEAD_DIM)] = mixed[:, h, :].astype(jnp.bfloat16)
    if columns is not None:
        held_copy.wait()


def attend(first, rows, arrays, after=None, weight=None, columns=None):
    draft, _, query_cols = arrays[2].shape
    _, cache_len, key_cols = arrays[5].shape
    heads = query_cols // HEAD_DIM
    vmem, anywhere = pl.BlockSpec(memory_space=pltpu.VMEM), pl.BlockSpec(memory_space=pl.ANY)
    tokens = [] if after is None else [after]
    given = [*arrays] if columns is None else [*arrays, weight]
    shapes = [jax.ShapeDtypeStruct((rows, query_cols), jnp.bfloat16)]
    if columns is not None:
        shapes.append(pltpu.VMEM((weight.shape[0], columns[1]), jnp.bfloat16))

    def kernel(*refs):
        attend_kernel(first, rows, columns, *refs[: len(given)], *refs[len(given) + len(tokens) :])

    return pl.pallas_call(
        kernel,
        out_shape=shapes,
        in_specs=[anywhere] * (len(given) + len(tokens)),
        out_specs=[vmem] * len(shapes),
        scratch_shapes=[
            pltpu.SMEM(arrays[0].shape, jnp.int32),
            pltpu.SMEM(arrays[1].shape, jnp.int32),
            pltpu.VMEM((draft, rows, query_cols), jnp.bfloat16),
            pltpu.VMEM((draft, rows, key_cols), jnp.bfloat16),
            pltpu.VMEM((draft, rows, key_cols), jnp.bfloat16),
            pltpu.VMEM((rows, cache_len, key_cols), jnp.bfloat16),
            pltpu.VMEM((rows, cache_len, key_cols), jnp.bfloat16),
            pltpu.VMEM((BLOCK, heads, HEAD_DIM), jnp.float32),
            pltpu.VMEM((BLOCK, heads, HEAD_DIM), jnp.float32),
            pltpu.SemaphoreType.DMA((5,)),
            pltpu.SemaphoreType.DMA((rows // CHUNK,)),
            pltpu.SemaphoreType.DMA((rows // CHUNK,)),
        ]
        + ([] if columns is None else [pltpu.SemaphoreType.DMA]),
        compiler_params=pltpu.CompilerParams(vmem_limit_bytes=8 << 20),
        cost_estimate=SHORT,
    )(*[pltpu.with_memory_space_constraint(a, pltpu.HBM) for a in given], *tokens)


def multiply_pieces(pieces, weights, part, features):
    at = 0
    for piece in pieces:
        features[pl.ds(at, piece.shape[0]), :] = piece[...]
        at += piece.shape[0]
    at = 0
    for weight in weights:
        for start in range(0, weight.shape[1], 512):
            tile = min(512, weight.shape[1] - start)
            product = jnp.dot(features[...], weight[:, pl.ds(start, tile)], preferred_element_type=jnp.float32)
            part[:, pl.ds(at + start, tile)] = product.astype(jnp.bfloat16)
        at += weight.shape[1]


def head(pieces, weights, after, works=None, otherwise=None):
    depth = weights[0].shape[0]
    rows = sum(piece.shape[0] for piece in pieces)
    cols = sum(weight.shape[1] for weight in weights)
    vmem, anywhere = pl.BlockSpec(memory_space=pltpu.VMEM), pl.BlockSpec(memory_space=pl.ANY)
    given = [*pieces, *[pltpu.with_memory_space_constraint(weight, pltpu.VMEM) for weight in weights]]
    given += [] if otherwise is None else [otherwise]

    def kernel(*refs):
        sides = refs[len(pieces) : len(pieces) + len(weights)]
        part, features = refs[-2:]
        if works is None:
            multiply_pieces(refs[: len(pieces)], sides, part, features)
        else:

            @pl.when(works())
            def _():
                multiply_pieces(refs[: len(pieces)], sides, part, features)

            if otherwise is not None:

                @pl.when(jnp.logical_not(works()))
                def _():
                    part[...] = refs[len(given) - 1][...]

    return pl.pallas_call(
        kernel,
        out_shape=jax.ShapeDtypeStruct((rows, cols), jnp.bfloat16),
        in_specs=[vmem] * len(given) + [anywhere],
        out_specs=vmem,
        scratch_shapes=[pltpu.VMEM((rows, depth), jnp.bfloat16)],
        compiler_params=pltpu.CompilerParams(vmem_limit_bytes=8 << 20),
        cost_estimate=SHORT,
    )(*given, after)


def swap(array, dp, bits):
    return lax.ppermute(array, "dp", [(i, i ^ bits) for i in range(dp)])


def behind(array, other):
    return lax.optimization_barrier((array, other))[0]


def shards(
    tensor, dp, queries, new_keys, new_values, key_cache, value_cache, cache_lengths, accepted, head_weight
):
    rows_dev = queries.shape[0]
    queries, new_keys, new_values = [jnp.transpose(a, (1, 0, 2)) for a in (queries, new_keys, new_values)]
    arrays = (cache_lengths, accepted, queries, new_keys, new_values, key_cache, value_cache)
    sources = dp // tensor
    paired = dp == 8 and tensor == 4
    cols = head_weight.shape[1]

    groups = rows_dev // BLOCK
    unit = cols // 8
    columns = [(0, 2 * unit), (2 * unit, 3 * unit), (5 * unit, 3 * unit)]
    first, weight = attend(0, BLOCK, arrays, None, head_weight, columns[0])
    blocks, weights, chips, pieces, last = [first], [weight], {}, {}, first
    for n in range(1, groups):
        if paired:
            chips[n - 1] = swap(blocks[n - 1], dp, 2)
        block, weight = attend(n * BLOCK, BLOCK, arrays, last, head_weight, columns[n])
        blocks.append(block)
        weights.append(weight)
        last = block
        if paired and n == 1:
            last = chips[0] = jnp.concatenate([first, behind(chips[0], block)])

    def along_y(n, after):
        chips[n] = jnp.concatenate([blocks[n], behind(chips[n], after)])

    def along_cores(n, after):
        both = jnp.concatenate([chips[n], behind(swap(chips[n], dp, 4), after)])
        pieces[n] = [both, swap(both, dp, 1)]

    def view(part):
        if paired:
            return part.reshape(2, tensor, -1, part.shape[-1])
        return part.reshape(1, tensor, -1, part.shape[-1])

    def chosen(shard):
        return shard ^ (lax.axis_index("dp") // 2) if paired else shard

    def add_kernel(parity, sources, *refs):
        *refs, sent = refs
        z = lax.axis_index("tensor")
        for n, (part, step, arrived, place) in enumerate(sources):
            shard = jnp.where(lax.rem(z, 2) == parity, tensor - step + z, step - tensor + z)
            at = chosen(jnp.clip(shard, 0, tensor - 1))
            if arrived is None:
                sent[n] = refs[part][:, at]
            else:
                total = refs[part][:, at].astype(jnp.float32) + refs[arrived][place].astype(jnp.float32)
                sent[n] = total.astype(jnp.bfloat16)

    def add(terms, parity, after):
        part = terms[0][0]
        shape = (len(terms), *part.shape[:1], *part.shape[2:])
        vmem = pl.BlockSpec(memory_space=pltpu.VMEM)
        given, sources = [], []
        for part, step, array, place in terms:
            sources.append((len(given), step, None if array is None else len(given) + 1, place))
            given += [part] if array is None else [part, array]
        return pl.pallas_call(
            lambda *refs: add_kernel(parity, sources, *refs[: len(given)], refs[-1]),
            out_shape=jax.ShapeDtypeStruct(shape, jnp.bfloat16),
            in_specs=[vmem] * len(given) + [pl.BlockSpec(memory_space=pl.ANY)],
            out_specs=vmem,
            compiler_params=pltpu.CompilerParams(vmem_limit_bytes=8 << 20),
            cost_estimate=SHORT,
        )(*given, after)

    def links(step, parity):
        up = [(z, z + 1) for z in range(parity, tensor - 1, 2) if z < step]
        down = [(z + 1, z) for z in range(parity, tensor - 1, 2) if tensor - 2 - z < step]
        return up + down

    parts, arrived, sums = {}, {}, {}

    def at_end():
        return (lax.axis_index("tensor") == 0) | (lax.axis_index("tensor") == tensor - 1)

    def multiply(n, after, works=None, otherwise=None):
        parts[n] = view(head(pieces[n], weights, after, works, otherwise))
        return parts[n]

    def send(entries, parity, after):
        terms = [(parts[n], step, *arrived.get((n, step - 1, 1 - parity), (None, None))) for n, step in entries]
        value = add(terms, parity, after)
        moved = lax.ppermute(value, "tensor", links(entries[0][1], parity))
        for place, (n, step) in enumerate(entries):
            arrived[n, step, parity] = moved, place
        return value

    def sum_kernel(first, rest):
        total = first[:, chosen(lax.axis_index("tensor"))].astype(jnp.float32) if len(first.shape) == 4 else first[...]
        for ref, place in rest:
            total = total + ref[place].astype(jnp.float32)
        return total

    def ended(n, parity):
        return [arrived[n, tensor - 1, parity]] if (n, tensor - 1, parity) in arrived else []

    def finish(n, parity, after):
        given = [sums.get(n, parts[n])] + [array for array, _ in ended(n, parity)]
        places = [place for _, place in ended(n, parity)]

        def kernel(*refs):
            refs[-1][...] = sum_kernel(refs[0], zip(refs[1 : len(given)], places))

        vmem = pl.BlockSpec(memory_space=pltpu.VMEM)
        sums[n] = pl.pallas_call(
            kernel,
            out_shape=jax.ShapeDtypeStruct(parts[n].shape[:1] + parts[n].shape[2:], jnp.float32),
            in_specs=[vmem] * len(given) + [pl.BlockSpec(memory_space=pl.ANY)],
            out_specs=vmem,
            compiler_params=pltpu.CompilerParams(vmem_limit_bytes=8 << 20),
            cost_estimate=SHORT,
        )(*given, after)
        return sums[n]

    def assemble():
        *earlier, part = [sums.get(n, parts[n]) for n in parts]
        came = ended(len(parts) - 1, 0) + ended(len(parts) - 1, 1)
        given = [part] + [array for array, _ in came]
        places = [place for _, place in came]

        def kernel(*refs):
            earlier, (part, *rest), out = refs[: len(parts) - 1], refs[len(parts) - 1 : -1], refs[-1]
            turned = lax.rem(lax.axis_index("dp"), 2) if paired else 0
            for n in range(len(parts)):
                total = earlier[n][...] if n < len(earlier) else sum_kernel(part, zip(rest, places))
                total = total.reshape(sources, BLOCK, cols)
                for source in range(sources):
                    out[source ^ turned, pl.ds(n * BLOCK, BLOCK)] = total[source]

        vmem = pl.BlockSpec(memory_space=pltpu.VMEM)
        out = pl.pallas_call(
            kernel,
            out_shape=jax.ShapeDtypeStruct((sources, len(parts) * BLOCK, cols), jnp.float32),
            in_specs=[vmem] * (len(earlier) + len(given)),
            out_specs=vmem,
            compiler_params=pltpu.CompilerParams(vmem_limit_bytes=16 << 20),
            cost_estimate=SHORT,
        )(*earlier, *given)
        return out.reshape(-1, cols)

    if paired:
        for step, *what in ORDER:
            if step == "beside":
                chips[what[0]] = swap(behind(blocks[what[0]], last), dp, 2)
            elif step == "below":
                along_y(what[0], last)
            elif step == "cores":
                along_cores(what[0], last)
            elif step == "ends":
                last = multiply(what[0], last, at_end)
            elif step == "between":
                last = multiply(what[0], last, lambda: ~at_end(), parts[what[0]].reshape(-1, cols))
            elif step == "head":
                last = multiply(what[0], last)
            elif step == "send":
                last = send(*what, last)
            else:
                last = finish(*what, last)
    else:
        for n, block in enumerate(blocks):
            pieces[n] = [lax.all_gather(block, "dp", axis=0, tiled=True)]
            last = multiply(n, last)
        for step in range(1, tensor):
            for n in range(len(blocks)):
                for parity in range(2):
                    if links(step, parity):
                        last = send([(n, step)], parity, last)

    for n in range(len(parts) - 1):
        if n not in sums:
            last = finish(n, 1, finish(n, 0, last))
    return assemble()


def solution(mesh):
    in_specs = (
        P("dp", None, "tensor"),
        P("dp", None, "tensor"),
        P("dp", None, "tensor"),
        P("dp", None, "tensor"),
        P("dp", None, "tensor"),
        P("dp"),
        P("dp"),
        P("tensor", "dp"),
    )
    out_specs = P("tensor", "dp")
    body = functools.partial(shards, mesh.shape["tensor"], mesh.shape["dp"])
    return jax.shard_map(body, mesh=mesh, in_specs=in_specs, out_specs=out_specs, check_vma=False)
```

```python
import functools

import jax
import jax.numpy as jnp
from jax import lax
from jax.experimental import pallas as pl
from jax.experimental.pallas import tpu as pltpu
from jax.sharding import PartitionSpec as P

HEAD_DIM = 128
BLOCK = 16
CHUNK = 16
LOWEST = -1e30
SHORT = pl.CostEstimate(flops=1, bytes_accessed=1, transcendentals=0)


ORDER = [
    ("cores", 0),
    ("below", 1),
    ("ends", 0),
    ("send", [(0, 1), (0, 2)], 0),
    ("between", 0),
    ("beside", 2),
    ("cores", 1),
    ("below", 2),
    ("head", 1),
    ("send", [(1, 1), (1, 2)], 0),
    ("send", [(0, 2), (0, 3)], 1),
    ("cores", 2),
    ("head", 2),
    ("send", [(2, 1)], 0),
    ("send", [(2, 2)], 0),
    ("send", [(1, 2)], 1),
    ("send", [(0, 3)], 0),
    ("send", [(2, 2)], 1),
    ("send", [(2, 3)], 1),
    ("send", [(1, 3)], 0),
    ("send", [(1, 3)], 1),
    ("finish", 0, 1),
    ("finish", 0, 0),
    ("send", [(2, 3)], 0),
    ("finish", 1, 1),
    ("finish", 1, 0),
]


def attend_kernel(first, rows, columns, *refs):
    all_lengths, all_accepted, queries, new_keys, new_values, key_cache, value_cache, *refs = refs
    if columns is None:
        picked, *scratch = refs
    else:
        weight, picked, held, *scratch, held_sem = refs
    lengths, accepted, q_buf, nk_buf, nv_buf, k_buf, v_buf, spread, mixed, small_sems, k_sems, v_sems = scratch
    draft, _, query_cols = q_buf.shape
    cache_len, key_cols = k_buf.shape[1:]
    groups, heads = key_cols // HEAD_DIM, query_cols // HEAD_DIM
    sharing = heads // groups
    scaling = HEAD_DIM ** (-0.5)
    own = pl.ds(first, rows)
    small = [(all_accepted, accepted), (all_lengths, lengths)]
    small += [(src.at[:, own], dst) for src, dst in ((queries, q_buf), (new_keys, nk_buf), (new_values, nv_buf))]
    small = [pltpu.make_async_copy(src, dst, small_sems.at[n]) for n, (src, dst) in enumerate(small)]
    keys, values = [
        [
            pltpu.make_async_copy(src.at[pl.ds(first + at, CHUNK)], dst.at[pl.ds(at, CHUNK)], sems.at[at // CHUNK])
            for at in range(0, rows, CHUNK)
        ]
        for src, dst, sems in ((key_cache, k_buf, k_sems), (value_cache, v_buf, v_sems))
    ]
    for copy in small:
        copy.start()
    for start in range(0, rows // CHUNK, BLOCK // CHUNK):
        for copy in keys[start : start + BLOCK // CHUNK] + values[start : start + BLOCK // CHUNK]:
            copy.start()
    if columns is not None:
        held_copy = pltpu.make_async_copy(weight.at[:, pl.ds(*columns)], held, held_sem)
        held_copy.start()
    for copy in small:
        copy.wait()
    lanes = BLOCK * heads
    nt, tn = (((1,), (1,)), ((), ())), (((0,), (0,)), ((), ()))
    lane_row = lax.broadcasted_iota(jnp.int32, (1, lanes), 1) // heads
    for block in range(0, rows, BLOCK):
        here = pl.ds(block, BLOCK)
        row = lax.broadcasted_iota(jnp.int32, (BLOCK, HEAD_DIM), 0)
        chosen = jnp.zeros((BLOCK, HEAD_DIM), jnp.int32)
        length, last = jnp.zeros((1, lanes), jnp.int32), jnp.zeros((1, lanes), jnp.int32)
        for r in range(BLOCK):
            chosen = jnp.where(row == r, accepted[first + block + r], chosen)
            last = jnp.where(lane_row == r, accepted[first + block + r], last)
            length = jnp.where(lane_row == r, lengths[first + block + r], length)
        for h in range(heads):
            cols = pl.ds(h * HEAD_DIM, HEAD_DIM)
            query = q_buf[0, here, cols].astype(jnp.float32)
            for p in range(1, draft):
                query = jnp.where(chosen == p, q_buf[p, here, cols].astype(jnp.float32), query)
            spread[:, h, :] = query
            wide = []
        for g in range(groups):
            keep = lax.broadcasted_iota(jnp.int32, spread.shape, 1) // sharing == g
            wide.append(jnp.where(keep, spread[...], 0.0).reshape(lanes, HEAD_DIM))
        query = jnp.concatenate(wide, axis=1).astype(jnp.bfloat16)

        fresh_keys = nk_buf[:, here, :].reshape(draft * BLOCK, key_cols)
        fresh_values = nv_buf[:, here, :].reshape(draft * BLOCK, key_cols)
        fresh = lax.dot_general(fresh_keys, query, nt, preferred_element_type=jnp.float32) * scaling
        slot = lax.broadcasted_iota(jnp.int32, fresh.shape, 0)
        fresh = jnp.where((slot % BLOCK == lane_row) & (slot // BLOCK <= last), fresh, LOWEST)
        past = []
        for lane in range(0, lanes, HEAD_DIM):
            part = None
            for r in range(lane // heads, (lane + HEAD_DIM) // heads):
                if r % CHUNK == 0:
                    keys[(block + r) // CHUNK].wait()
                score = lax.dot_general(
                    k_buf[block + r], query[lane : lane + HEAD_DIM], nt, preferred_element_type=jnp.float32
                )
                part = score if part is None else jnp.where(lane_row[:, lane : lane + HEAD_DIM] == r, score, part)
            past.append(part)
        past = jnp.concatenate(past, axis=1) * scaling
        past = jnp.where(lax.broadcasted_iota(jnp.int32, past.shape, 0) < length, past, LOWEST)
        peak = jnp.maximum(jnp.max(past, axis=0, keepdims=True), jnp.max(fresh, axis=0, keepdims=True))
        past, fresh = jnp.exp(past - peak), jnp.exp(fresh - peak)
        total = jnp.sum(past, axis=0, keepdims=True) + jnp.sum(fresh, axis=0, keepdims=True)
        weights = jnp.transpose(past / total)
        fresh = (fresh / total).astype(jnp.bfloat16)
        fresh = lax.dot_general(fresh, fresh_values, tn, preferred_element_type=jnp.float32)
        own_group = lax.broadcasted_iota(jnp.int32, (heads, HEAD_DIM), 0) // sharing
        for r in range(BLOCK):
            if r % CHUNK == 0:
                values[(block + r) // CHUNK].wait()
            mine = slice(r * heads, (r + 1) * heads)
            result = jnp.dot(weights[mine].astype(jnp.bfloat16), v_buf[block + r], preferred_element_type=jnp.float32)
            result = result + fresh[mine]
            kept = result[:, :HEAD_DIM]
            for g in range(1, groups):
                kept = jnp.where(own_group == g, result[:, g * HEAD_DIM : (g + 1) * HEAD_DIM], kept)
            mixed[r] = kept
        for h in range(heads):
            picked[here, pl.ds(h * HEAD_DIM, HEAD_DIM)] = mixed[:, h, :].astype(jnp.bfloat16)
    if columns is not None:
        held_copy.wait()


def attend(first, rows, arrays, after=None, weight=None, columns=None):
    draft, _, query_cols = arrays[2].shape
    _, cache_len, key_cols = arrays[5].shape
    heads = query_cols // HEAD_DIM
    vmem, anywhere = pl.BlockSpec(memory_space=pltpu.VMEM), pl.BlockSpec(memory_space=pl.ANY)
    tokens = [] if after is None else [after]
    given = [*arrays] if columns is None else [*arrays, weight]
    shapes = [jax.ShapeDtypeStruct((rows, query_cols), jnp.bfloat16)]
    if columns is not None:
        shapes.append(pltpu.VMEM((weight.shape[0], columns[1]), jnp.bfloat16))

    def kernel(*refs):
        attend_kernel(first, rows, columns, *refs[: len(given)], *refs[len(given) + len(tokens) :])

    return pl.pallas_call(
        kernel,
        out_shape=shapes,
        in_specs=[anywhere] * (len(given) + len(tokens)),
        out_specs=[vmem] * len(shapes),
        scratch_shapes=[
            pltpu.SMEM(arrays[0].shape, jnp.int32),
            pltpu.SMEM(arrays[1].shape, jnp.int32),
            pltpu.VMEM((draft, rows, query_cols), jnp.bfloat16),
            pltpu.VMEM((draft, rows, key_cols), jnp.bfloat16),
            pltpu.VMEM((draft, rows, key_cols), jnp.bfloat16),
            pltpu.VMEM((rows, cache_len, key_cols), jnp.bfloat16),
            pltpu.VMEM((rows, cache_len, key_cols), jnp.bfloat16),
            pltpu.VMEM((BLOCK, heads, HEAD_DIM), jnp.float32),
            pltpu.VMEM((BLOCK, heads, HEAD_DIM), jnp.float32),
            pltpu.SemaphoreType.DMA((5,)),
            pltpu.SemaphoreType.DMA((rows // CHUNK,)),
            pltpu.SemaphoreType.DMA((rows // CHUNK,)),
        ]
        + ([] if columns is None else [pltpu.SemaphoreType.DMA]),
        compiler_params=pltpu.CompilerParams(vmem_limit_bytes=8 << 20),
        cost_estimate=SHORT,
    )(*[pltpu.with_memory_space_constraint(a, pltpu.HBM) for a in given], *tokens)


def multiply_pieces(pieces, weights, part, features):
    at = 0
    for piece in pieces:
        features[pl.ds(at, piece.shape[0]), :] = piece[...]
        at += piece.shape[0]
    at = 0
    for weight in weights:
        for start in range(0, weight.shape[1], 512):
            tile = min(512, weight.shape[1] - start)
            product = jnp.dot(features[...], weight[:, pl.ds(start, tile)], preferred_element_type=jnp.float32)
            part[:, pl.ds(at + start, tile)] = product.astype(jnp.bfloat16)
        at += weight.shape[1]


def head(pieces, weights, after, works=None, otherwise=None):
    depth = weights[0].shape[0]
    rows = sum(piece.shape[0] for piece in pieces)
    cols = sum(weight.shape[1] for weight in weights)
    vmem, anywhere = pl.BlockSpec(memory_space=pltpu.VMEM), pl.BlockSpec(memory_space=pl.ANY)
    given = [*pieces, *[pltpu.with_memory_space_constraint(weight, pltpu.VMEM) for weight in weights]]
    given += [] if otherwise is None else [otherwise]

    def kernel(*refs):
        sides = refs[len(pieces) : len(pieces) + len(weights)]
        part, features = refs[-2:]
        if works is None:
            multiply_pieces(refs[: len(pieces)], sides, part, features)
        else:

            @pl.when(works())
            def _():
                multiply_pieces(refs[: len(pieces)], sides, part, features)

            if otherwise is not None:

                @pl.when(jnp.logical_not(works()))
                def _():
                    part[...] = refs[len(given) - 1][...]

    return pl.pallas_call(
        kernel,
        out_shape=jax.ShapeDtypeStruct((rows, cols), jnp.bfloat16),
        in_specs=[vmem] * len(given) + [anywhere],
        out_specs=vmem,
        scratch_shapes=[pltpu.VMEM((rows, depth), jnp.bfloat16)],
        compiler_params=pltpu.CompilerParams(vmem_limit_bytes=8 << 20),
        cost_estimate=SHORT,
    )(*given, after)


def swap(array, dp, bits):
    return lax.ppermute(array, "dp", [(i, i ^ bits) for i in range(dp)])


def behind(array, other):
    return lax.optimization_barrier((array, other))[0]


def shards(
    tensor, dp, queries, new_keys, new_values, key_cache, value_cache, cache_lengths, accepted, head_weight
):
    rows_dev = queries.shape[0]
    queries, new_keys, new_values = [jnp.transpose(a, (1, 0, 2)) for a in (queries, new_keys, new_values)]
    arrays = (cache_lengths, accepted, queries, new_keys, new_values, key_cache, value_cache)
    sources = dp // tensor
    paired = dp == 8 and tensor == 4
    cols = head_weight.shape[1]

    groups = rows_dev // BLOCK
    unit = cols // 8
    columns = [(0, 2 * unit), (2 * unit, 3 * unit), (5 * unit, 3 * unit)]
    first, weight = attend(0, BLOCK, arrays, None, head_weight, columns[0])
    blocks, weights, chips, pieces, last = [first], [weight], {}, {}, first
    for n in range(1, groups):
        if paired:
            chips[n - 1] = swap(blocks[n - 1], dp, 2)
        block, weight = attend(n * BLOCK, BLOCK, arrays, last, head_weight, columns[n])
        blocks.append(block)
        weights.append(weight)
        last = block
        if paired and n == 1:
            last = chips[0] = jnp.concatenate([first, behind(chips[0], block)])

    def along_y(n, after):
        chips[n] = jnp.concatenate([blocks[n], behind(chips[n], after)])

    def along_cores(n, after):
        both = jnp.concatenate([chips[n], behind(swap(chips[n], dp, 4), after)])
        pieces[n] = [both, swap(both, dp, 1)]

    def view(part):
        if paired:
            return part.reshape(2, tensor, -1, part.shape[-1])
        return part.reshape(1, tensor, -1, part.shape[-1])

    def chosen(shard):
        return shard ^ (lax.axis_index("dp") // 2) if paired else shard

    def add_kernel(parity, sources, *refs):
        *refs, sent = refs
        z = lax.axis_index("tensor")
        for n, (part, step, arrived, place) in enumerate(sources):
            shard = jnp.where(lax.rem(z, 2) == parity, tensor - step + z, step - tensor + z)
            at = chosen(jnp.clip(shard, 0, tensor - 1))
            if arrived is None:
                sent[n] = refs[part][:, at]
            else:
                total = refs[part][:, at].astype(jnp.float32) + refs[arrived][place].astype(jnp.float32)
                sent[n] = total.astype(jnp.bfloat16)

    def add(terms, parity, after):
        part = terms[0][0]
        shape = (len(terms), *part.shape[:1], *part.shape[2:])
        vmem = pl.BlockSpec(memory_space=pltpu.VMEM)
        given, sources = [], []
        for part, step, array, place in terms:
            sources.append((len(given), step, None if array is None else len(given) + 1, place))
            given += [part] if array is None else [part, array]
        return pl.pallas_call(
            lambda *refs: add_kernel(parity, sources, *refs[: len(given)], refs[-1]),
            out_shape=jax.ShapeDtypeStruct(shape, jnp.bfloat16),
            in_specs=[vmem] * len(given) + [pl.BlockSpec(memory_space=pl.ANY)],
            out_specs=vmem,
            compiler_params=pltpu.CompilerParams(vmem_limit_bytes=8 << 20),
            cost_estimate=SHORT,
        )(*given, after)

    def links(step, parity):
        up = [(z, z + 1) for z in range(parity, tensor - 1, 2) if z < step]
        down = [(z + 1, z) for z in range(parity, tensor - 1, 2) if tensor - 2 - z < step]
        return up + down

    parts, arrived, sums = {}, {}, {}

    def at_end():
        return (lax.axis_index("tensor") == 0) | (lax.axis_index("tensor") == tensor - 1)

    def multiply(n, after, works=None, otherwise=None):
        parts[n] = view(head(pieces[n], weights, after, works, otherwise))
        return parts[n]

    def send(entries, parity, after):
        terms = [(parts[n], step, *arrived.get((n, step - 1, 1 - parity), (None, None))) for n, step in entries]
        value = add(terms, parity, after)
        moved = lax.ppermute(value, "tensor", links(entries[0][1], parity))
        for place, (n, step) in enumerate(entries):
            arrived[n, step, parity] = moved, place
        return value

    def sum_kernel(first, rest):
        total = first[:, chosen(lax.axis_index("tensor"))].astype(jnp.float32) if len(first.shape) == 4 else first[...]
        for ref, place in rest:
            total = total + ref[place].astype(jnp.float32)
        return total

    def ended(n, parity):
        return [arrived[n, tensor - 1, parity]] if (n, tensor - 1, parity) in arrived else []

    def finish(n, parity, after):
        given = [sums.get(n, parts[n])] + [array for array, _ in ended(n, parity)]
        places = [place for _, place in ended(n, parity)]

        def kernel(*refs):
            refs[-1][...] = sum_kernel(refs[0], zip(refs[1 : len(given)], places))

        vmem = pl.BlockSpec(memory_space=pltpu.VMEM)
        sums[n] = pl.pallas_call(
            kernel,
            out_shape=jax.ShapeDtypeStruct(parts[n].shape[:1] + parts[n].shape[2:], jnp.float32),
            in_specs=[vmem] * len(given) + [pl.BlockSpec(memory_space=pl.ANY)],
            out_specs=vmem,
            compiler_params=pltpu.CompilerParams(vmem_limit_bytes=8 << 20),
            cost_estimate=SHORT,
        )(*given, after)
        return sums[n]

    def assemble():
        *earlier, part = [sums.get(n, parts[n]) for n in parts]
        came = ended(len(parts) - 1, 0) + ended(len(parts) - 1, 1)
        given = [part] + [array for array, _ in came]
        places = [place for _, place in came]

        earlier = [array.reshape(sources, BLOCK, cols) for array in earlier]

        def kernel(*refs):
            earlier, (part, *rest), (out, total, sems) = refs[: len(parts) - 1], refs[len(parts) - 1 : -3], refs[-3:]
            turned = lax.rem(lax.axis_index("dp"), 2) if paired else 0
            copies = [
                pltpu.make_async_copy(array.at[source], out.at[source ^ turned, pl.ds(n * BLOCK, BLOCK)], sems.at[n, source])
                for n, array in enumerate((*earlier, total))
                for source in range(sources)
            ]
            for copy in copies[:-sources]:
                copy.start()
            total[...] = sum_kernel(part, zip(rest, places)).reshape(sources, BLOCK, cols)
            for copy in copies[-sources:]:
                copy.start()
            for copy in copies:
                copy.wait()

        vmem = pl.BlockSpec(memory_space=pltpu.VMEM)
        out = pl.pallas_call(
            kernel,
            out_shape=jax.ShapeDtypeStruct((sources, len(parts) * BLOCK, cols), jnp.float32),
            in_specs=[vmem] * (len(earlier) + len(given)),
            out_specs=pl.BlockSpec(memory_space=pl.ANY),
            scratch_shapes=[
                pltpu.VMEM((sources, BLOCK, cols), jnp.float32),
                pltpu.SemaphoreType.DMA((len(parts), sources)),
            ],
            compiler_params=pltpu.CompilerParams(vmem_limit_bytes=16 << 20),
            cost_estimate=SHORT,
        )(*earlier, *given)
        return out.reshape(-1, cols)

    if paired:
        for step, *what in ORDER:
            if step == "beside":
                chips[what[0]] = swap(behind(blocks[what[0]], last), dp, 2)
            elif step == "below":
                along_y(what[0], last)
            elif step == "cores":
                along_cores(what[0], last)
            elif step == "ends":
                last = multiply(what[0], last, at_end)
            elif step == "between":
                last = multiply(what[0], last, lambda: ~at_end(), parts[what[0]].reshape(-1, cols))
            elif step == "head":
                last = multiply(what[0], last)
            elif step == "send":
                last = send(*what, last)
            else:
                last = finish(*what, last)
    else:
        for n, block in enumerate(blocks):
            pieces[n] = [lax.all_gather(block, "dp", axis=0, tiled=True)]
            last = multiply(n, last)
        for step in range(1, tensor):
            for n in range(len(blocks)):
                for parity in range(2):
                    if links(step, parity):
                        last = send([(n, step)], parity, last)

    for n in range(len(parts) - 1):
        if n not in sums:
            last = finish(n, 1, finish(n, 0, last))
    return assemble()


def solution(mesh):
    in_specs = (
        P("dp", None, "tensor"),
        P("dp", None, "tensor"),
        P("dp", None, "tensor"),
        P("dp", None, "tensor"),
        P("dp", None, "tensor"),
        P("dp"),
        P("dp"),
        P("tensor", "dp"),
    )
    out_specs = P("tensor", "dp")
    body = functools.partial(shards, mesh.shape["tensor"], mesh.shape["dp"])
    return jax.shard_map(body, mesh=mesh, in_specs=in_specs, out_specs=out_specs, check_vma=False)
```
